32 devices in a mesh: seq: 4 (over z), batch: 8 (over y, x, core).
Axes of the slice: x: 2, y: 2, z: 4, core: 2. Of those that a mesh axis runs over, the one named last changes fastest.
Arguments:
- dt_raw: float32 [8, 512, 40], P('batch', 'seq'), may hold values from -6 to 64
- dt_bias: float32 [40], replicated, may hold values from -2.5 to -1
- a_log: float32 [40], replicated, may hold values from -10 to -1
- d_skip: float32 [40], replicated, may hold values from 0.5 to 1.5
- x_in: bfloat16 [8, 512, 2560], P('batch', 'seq'), may hold values from -6 to 6
- b_in: bfloat16 [8, 512, 128], P('batch', 'seq'), may hold values from -1.796875 to 1.796875
- c_in: bfloat16 [8, 512, 128], P('batch', 'seq'), may hold values from -0.52734375 to 0.52734375
- cotangent: bfloat16 [8, 512, 2560], P('batch', 'seq'), may hold values from -6 to 6
Outputs:
- layer_out: bfloat16 [8, 512, 2560], P('batch', 'seq')
- grad_x: bfloat16 [8, 512, 2560], P('batch', 'seq')
- grad_b: bfloat16 [8, 512, 128], P('batch', 'seq')
- grad_c: bfloat16 [8, 512, 128], P('batch', 'seq')
- grad_dt_raw: float32 [8, 512, 40], P('batch', 'seq')
- grad_a_log: float32 [40], replicated
- grad_dt_bias: float32 [40], replicated
- grad_d_skip: float32 [40], replicated
The draws below stay inside these ranges and needn't reach their ends.
All inputs are finite; a program needn't handle non-finite values.
Results may differ from the reference program's by a relative error of at most 0.024.
Values may be sent and summed in bfloat16 or wider, within the bound.
A program may use at most 64 MiB of HBM per device.

```python
import jax
import jax.numpy as jnp
from jax import lax

PAIRED_GROUPS = 40
HEAD_DIM = 64
STATE = 128
TOK_DEV = 128
CHANNELS = 2560
STRING_SPAN = 512
NUM_STRINGS = 8
N_SEQ = 4


def draw_dt_raw(key, part):
    key_base = jax.random.fold_in(key, 11)
    key_spot = jax.random.fold_in(key, 12)
    key_scale = jax.random.fold_in(key, 13)
    key_hit = jax.random.fold_in(key, 14)
    blocks = STRING_SPAN // TOK_DEV
    starting_number = jnp.clip(jax.random.normal(key_base, (NUM_STRINGS, STRING_SPAN, PAIRED_GROUPS), jnp.float32) * 1.4, -6.0, 3.5)
    spot_offsets = jax.random.randint(key_spot, (NUM_STRINGS, blocks), 0, TOK_DEV)
    spot_rows = jnp.repeat(spot_offsets, TOK_DEV, axis=1)
    offsets = jnp.arange(STRING_SPAN) % TOK_DEV
    spot_mask = offsets[None, :] == spot_rows
    share = min(1.0, 2.0 / blocks)
    head_first = (jnp.arange(PAIRED_GROUPS) == 0)[None, None, :]
    block_first = (jnp.arange(blocks) == 0)[None, :, None]
    forced = head_first & block_first
    hit_heads = (jax.random.uniform(key_hit, (NUM_STRINGS, blocks, PAIRED_GROUPS), jnp.float32) < share) | forced
    factor = jax.random.uniform(key_scale, (NUM_STRINGS, blocks, PAIRED_GROUPS), jnp.float32, 0.8, 1.0)
    factor = jnp.where(forced, jnp.float32(1.0), factor)
    hit_rows = jnp.repeat(hit_heads, TOK_DEV, axis=1)
    factor_rows = jnp.repeat(factor, TOK_DEV, axis=1)
    spike_magnitude = factor_rows * jnp.float32(STRING_SPAN // 8)
    chosen = spot_mask[:, :, None] & hit_rows
    return jnp.where(chosen, spike_magnitude, starting_number).astype(jnp.float32)


def draw_a_log(key, part):
    key_pick = jax.random.fold_in(key, 31)
    key_slow = jax.random.fold_in(key, 32)
    key_fast = jax.random.fold_in(key, 33)
    share = 0.5
    fast_heads = jax.random.uniform(key_pick, (PAIRED_GROUPS,), jnp.float32) < share
    slow_rate = jnp.exp(jax.random.uniform(key_slow, (PAIRED_GROUPS,), jnp.float32, jnp.log(1.5 / STRING_SPAN), jnp.log(4.0 / STRING_SPAN)))
    fast_rate = jnp.exp(jax.random.uniform(key_fast, (PAIRED_GROUPS,), jnp.float32, jnp.log(0.1), jnp.log(0.17)))
    return jnp.log(jnp.where(fast_heads, fast_rate, slow_rate)).astype(jnp.float32)


def steps_of(key, shape, shards, low, largest):
    def one(dim, shards_of):
        draws = jax.random.uniform(jax.random.fold_in(jax.random.fold_in(key, 6), dim), (shards_of,), jnp.float32, low / len(shards), largest / len(shards))
        return jnp.repeat(jnp.exp(draws), shape[dim] // shards_of).reshape((-1,) + (1,) * (len(shape) - dim - 1))

    level = one(*shards[0])
    for cut in shards[1:]:
        level = level * one(*cut)
    return level


def centred(rng, dims, width, most, cuts=(), dtype=jnp.bfloat16):
    level = steps_of(rng, dims, cuts, -0.22, 0.18) if cuts else 1.0
    array = jax.random.normal(rng, dims, jnp.float32) * width * level
    return jnp.minimum(jnp.maximum(array, -most), most).astype(dtype)


def setup_inputs(seed: int = 0) -> dict:
    key_list = jax.random.split(jax.random.key(seed), 9)
    dt_raw = draw_dt_raw(jax.random.fold_in(key_list[8], 71), 0)
    dt_bias = jnp.clip(jax.random.uniform(key_list[1], (PAIRED_GROUPS,), jnp.float32, -2.5, -1.0), -2.5, -1.0)
    a_log = draw_a_log(jax.random.fold_in(key_list[8], 71), 0)
    d_skip = jnp.clip(jax.random.uniform(key_list[3], (PAIRED_GROUPS,), jnp.float32, 0.5, 1.5), 0.5, 1.5)
    x_in = centred(key_list[4], (NUM_STRINGS, STRING_SPAN, CHANNELS), 1.0, 6.0, ((0, 8), (1, 4)))
    b_in = centred(key_list[5], (NUM_STRINGS, STRING_SPAN, STATE), 0.3, 1.796875, ((0, 8), (1, 4)))
    c_in = centred(key_list[6], (NUM_STRINGS, STRING_SPAN, STATE), (STATE ** -0.5), 0.52734375, ((0, 8), (1, 4)))
    cotangent = centred(key_list[7], (NUM_STRINGS, STRING_SPAN, CHANNELS), 1.0, 6.0, ((0, 8), (1, 4)))
    return dict(dt_raw=dt_raw, dt_bias=dt_bias, a_log=a_log, d_skip=d_skip, x_in=x_in, b_in=b_in, c_in=c_in, cotangent=cotangent)


def step_terms(dt_raw, a_log, dt_bias):
    step_size = jax.nn.softplus(dt_raw + dt_bias[None, :])
    decay_log = -jnp.exp(a_log)[None, :] * step_size
    cum_log = jnp.cumsum(decay_log, axis=0)
    return (step_size, cum_log)

def block_state(dt_raw, a_log, dt_bias, x_rows, b_rows):
    step_size, cum_log = step_terms(dt_raw, a_log, dt_bias)
    last_cum = cum_log[-1]
    weight = jnp.exp(last_cum[None, :] - cum_log) * step_size
    weighted = (weight.T[:, :, None] * b_rows.astype(jnp.float32)[None, :, :]).astype(jnp.bfloat16)
    x_heads = x_rows.reshape(x_rows.shape[0], a_log.shape[0], HEAD_DIM)
    state_sum = jnp.einsum('thp,htn->hpn', x_heads.astype(jnp.float32), weighted.astype(jnp.float32))
    return (last_cum.astype(jnp.bfloat16), state_sum.astype(jnp.bfloat16))

def block_output(dt_raw, a_log, dt_bias, d_skip, x_rows, b_rows, c_rows, carried):
    step_size, cum_log = step_terms(dt_raw, a_log, dt_bias)
    length = x_rows.shape[0]
    x_heads = x_rows.reshape(length, a_log.shape[0], HEAD_DIM).astype(jnp.float32)
    cb_inner = jnp.dot(c_rows, b_rows.T, preferred_element_type=jnp.float32)
    positions = jnp.arange(length)
    causal = (positions[:, None] >= positions[None, :])[None]
    log_gap = cum_log.T[:, :, None] - cum_log.T[:, None, :]
    decay_gate = jnp.exp(jnp.where(causal, log_gap, 0.0)) * step_size.T[:, None, :]
    scores = jnp.where(causal, decay_gate * cb_inner[None], 0.0).astype(jnp.bfloat16)
    intra_part = jnp.einsum('hts,shp->thp', scores.astype(jnp.float32), x_heads)
    inter_part = jnp.einsum('tn,hpn->thp', c_rows.astype(jnp.float32), carried.astype(jnp.float32))
    inter_part = inter_part * jnp.exp(cum_log)[:, :, None]
    result = intra_part + inter_part + d_skip[None, :, None] * x_heads
    return result.reshape(length, -1)

def sequence_output(a_log, dt_bias, d_skip, x_rows, b_rows, c_rows, dt_raw):
    running = jnp.zeros((a_log.shape[0], HEAD_DIM, b_rows.shape[1]), jnp.float32)
    pieces = []
    for block_idx in range(N_SEQ):
        low = block_idx * TOK_DEV
        high = low + TOK_DEV
        decay_log, local_state = block_state(dt_raw[low:high], a_log, dt_bias, x_rows[low:high], b_rows[low:high])
        pieces.append(block_output(dt_raw[low:high], a_log, dt_bias, d_skip, x_rows[low:high], b_rows[low:high], c_rows[low:high], running.astype(jnp.bfloat16)))
        running = jnp.exp(decay_log.astype(jnp.float32))[:, None, None] * running + local_state.astype(jnp.float32)
    return jnp.concatenate(pieces, axis=0)

def reference(dt_raw, dt_bias, a_log, d_skip, x_in, b_in, c_in, cotangent):

    def one_sequence(members):
        dt_rows, x_rows, b_rows, c_rows, cot_rows = members
        output_f32, pullback = jax.vjp(sequence_output, a_log, dt_bias, d_skip, x_rows, b_rows, c_rows, dt_rows)
        grads = pullback(cot_rows.astype(jnp.float32))
        return (output_f32.astype(jnp.bfloat16), grads[3].astype(jnp.bfloat16), grads[4].astype(jnp.bfloat16), grads[5].astype(jnp.bfloat16), grads[6], grads[0], grads[1], grads[2])
    results = lax.map(one_sequence, (dt_raw, x_in, b_in, c_in, cotangent))
    return (results[0], results[1], results[2], results[3], results[4], lax.optimization_barrier(jnp.sum(results[5], axis=0)), lax.optimization_barrier(jnp.sum(results[6], axis=0)), lax.optimization_barrier(jnp.sum(results[7], axis=0)))
```

```python
import functools

import jax
import jax.numpy as jnp
from jax import lax
from jax.experimental import pallas as pl
from jax.experimental.pallas import tpu as pltpu
from jax.sharding import PartitionSpec as P

HEAD_DIM = 64
WIDTH = 256
LAG = 3
FLAT = 64
LOG2E = 1.4426950408889634
F32 = jnp.float32
BF16 = jnp.bfloat16


def mm(a, b):
    return jnp.dot(a, b, preferred_element_type=F32)


def mm_nt(a, b):
    return lax.dot_general(a, b, (((1,), (1,)), ((), ())), preferred_element_type=F32)


def exact(a, b):
    return jnp.dot(a, b, preferred_element_type=F32, precision=lax.Precision.HIGHEST)


def iota(shape, dim):
    return lax.broadcasted_iota(jnp.int32, shape, dim)


def split3(value, heads):
    high = value.astype(BF16).astype(F32)
    rest = value - high
    mid = rest.astype(BF16).astype(F32)
    low = (rest - mid).astype(BF16).astype(F32)
    packed = high + pltpu.roll(mid, heads, 1) + pltpu.roll(low, 2 * heads, 1)
    return packed.astype(BF16)


def kernel(
    n, m, heads, tokens,
    dt_hbm, bias_hbm, alog_hbm, skip_hbm, x_hbm, b_hbm, c_hbm, g_hbm,
    out_ref, gx_ref, gb_ref, gc_ref, gdt_ref, ga_out, gbias_out, gskip_out,
    dt_ref, bias_ref, alog_ref, skip_ref, x_ref, b_ref, c_ref, g_ref,
    in_sem, pad, prm, pk, apk, vt, kmod, cbm, ms, ee, we, wx, eg, sl, dc, vin, uin,
    fsend, car, bsend, ds,
    rowa, cola, misc, dcb, gba, gca, reds, redb,
    fs_sem, fr_sem, bs_sem, br_sem, rs_send, rs_recv, rb_send, rb_recv,
):
    z = lax.axis_index("seq")
    w = lax.axis_index("batch")
    chunks = heads * HEAD_DIM // WIDTH
    per = WIDTH // HEAD_DIM

    fetches = [
        pltpu.make_async_copy(a, b, in_sem.at[i])
        for i, (a, b) in enumerate((
            (dt_hbm, dt_ref), (bias_hbm, bias_ref), (alog_hbm, alog_ref), (skip_hbm, skip_ref),
            (b_hbm, b_ref), (c_hbm, c_ref), (x_hbm, x_ref), (g_hbm, g_ref)))
    ]
    for fetch in fetches:
        fetch.start()
    barrier = pltpu.get_barrier_semaphore()

    def other(d):
        place = lax.rem(z * m + w + d, n * m)
        return {"seq": lax.div(place, m), "batch": lax.rem(place, m)}

    def greet_seq(d, _):
        pl.semaphore_signal(barrier, inc=1, device_id={"seq": lax.rem(z + d, n)},
                            device_id_type=pl.DeviceIdType.MESH)
        return 0

    def greet_batch(d, _):
        pl.semaphore_signal(barrier, inc=1, device_id={"batch": lax.rem(w + d, m)},
                            device_id_type=pl.DeviceIdType.MESH)
        return 0

    def greet_all(d, _):
        pl.semaphore_signal(barrier, inc=1, device_id=other(d),
                            device_id_type=pl.DeviceIdType.MESH)
        return 0

    flat = n * m <= FLAT
    peers = n * m - 1 if flat else n + m - 2
    if flat:
        lax.fori_loop(1, n * m, greet_all, 0)
    else:
        lax.fori_loop(1, n, greet_seq, 0)
        lax.fori_loop(1, m, greet_batch, 0)

    def fcopy(i):
        return pltpu.make_async_remote_copy(
            src_ref=fsend.at[i], dst_ref=car.at[i], send_sem=fs_sem.at[i], recv_sem=fr_sem.at[i],
            device_id={"seq": jnp.minimum(z + 1, n - 1)}, device_id_type=pl.DeviceIdType.MESH)

    def bcopy(i):
        return pltpu.make_async_remote_copy(
            src_ref=bsend.at[i], dst_ref=ds.at[i], send_sem=bs_sem.at[i], recv_sem=br_sem.at[i],
            device_id={"seq": jnp.maximum(z - 1, 0)}, device_id_type=pl.DeviceIdType.MESH)

    pad[...] = jnp.zeros_like(pad)
    prm[...] = jnp.zeros_like(prm)
    for fetch in fetches[:6]:
        fetch.wait()
    pad[0:heads, :] = dt_ref[...]
    prm[0:1, :heads] = bias_ref[...]
    prm[1:2, :heads] = alog_ref[...]
    prm[2:3, :heads] = skip_ref[...]
    square = (tokens, tokens)
    is_head = iota(square, 1) < heads
    raw = pad[...].T + prm[0:1, :]
    step = jnp.maximum(raw, 0.0) + jnp.log1p(jnp.exp(-jnp.abs(raw)))
    rate = jnp.exp(prm[1:2, :])
    decay = jnp.where(is_head, -rate * step, 0.0)
    causal = iota(square, 0) >= iota(square, 1)
    cum = exact(jnp.where(causal, 1.0, 0.0), decay)
    last = cum[tokens - 1 : tokens, :]
    pk[0:tokens, :] = split3(jnp.where(is_head, jnp.exp(cum), 0.0), heads)
    pk[tokens : 2 * tokens, :] = split3(
        jnp.where(is_head, jnp.exp(last - cum) * step, 0.0), heads)
    head_row = is_head[0:1, :]
    factor = jnp.where(head_row, jnp.exp(last.astype(BF16).astype(F32)), 0.0)
    row16 = iota((16, tokens), 0)
    pk[2 * tokens : 2 * tokens + 16, :] = split3(
        jnp.where(row16 == 0, prm[2:3, :], 0.0) + jnp.where(row16 == 1, factor, 0.0), heads)
    k = iota((tokens, WIDTH), 0)
    kmod[...] = k - jnp.where(k >= heads, heads, 0) - jnp.where(k >= 2 * heads, heads, 0)
    b16 = b_ref[...]
    c16 = c_ref[...]
    bt = b16.astype(F32).T.astype(BF16)
    ct = c16.astype(F32).T.astype(BF16)

    for fetch in fetches[6:]:
        fetch.wait()
    pl.semaphore_wait(barrier, peers)

    def cols(i):
        return pl.ds(pl.multiple_of(i * WIDTH, WIDTH), WIDTH)

    def states(i, _):
        group = lax.shift_right_logical(iota((tokens, WIDTH), 1), 6)
        spread = jnp.where(kmod[...] - group == i * per, 1.0, 0.0).astype(BF16)
        wide = mm(pk[...], spread)
        ee[i] = wide[0:tokens]
        we[i] = wide[tokens : 2 * tokens]
        ms[i] = wide[2 * tokens : 2 * tokens + 8]
        wx_i = (x_ref[:, cols(i)].astype(F32) * wide[tokens : 2 * tokens]).astype(BF16)
        eg_i = (g_ref[:, cols(i)].astype(F32) * wide[0:tokens]).astype(BF16)
        wx[i] = wx_i
        eg[i] = eg_i
        sl_i = mm(bt, wx_i)
        dc_i = mm(ct, eg_i)
        sl[i] = sl_i
        dc[i] = dc_i

        @pl.when(z == 0)
        def _():
            car[i] = jnp.zeros((tokens, WIDTH), BF16)
            fsend[i] = sl_i.astype(BF16)
            fcopy(i).start()

        @pl.when(z == n - 1)
        def _():
            ds[i] = jnp.zeros((tokens, WIDTH), BF16)
            bsend[i] = dc_i.astype(BF16)
            bcopy(i).start()

        return 0

    lax.fori_loop(0, chunks, states, 0)

    cum2 = cum * LOG2E
    apk[...] = split3(cum2, heads)
    vt[...] = (cum2 - jnp.log(step) * LOG2E).T
    cbm[...] = jnp.where(causal, mm(c16, bt), 0.0)
    for acc in (rowa, cola, misc, dcb, gba, gca):
        acc[...] = jnp.zeros_like(acc)

    def to_heads(value, i):
        group = lax.shift_right_logical(iota((WIDTH, tokens), 0), 6)
        gather = jnp.where(iota((WIDTH, tokens), 1) - group == i * per, 1.0, 0.0).astype(BF16)
        high = value.astype(BF16)
        low = (value - high.astype(F32)).astype(BF16)
        return mm(high, gather) + mm(low, gather)

    def within(i):
        lane = iota(square, 1)
        left = jnp.where(lane < HEAD_DIM, 1.0, 0.0).astype(BF16)
        right = jnp.where(lane < HEAD_DIM, 0.0, 1.0).astype(BF16)
        second = jnp.where(iota((tokens, 2 * tokens), 1) < tokens, 0, 1)
        table = kmod[:, 0:1] - second
        cb2 = jnp.concatenate([cbm[...], cbm[...]], axis=1)
        for q in range(WIDTH // 128):
            head = i * per + 2 * q
            pair = pl.ds(pl.multiple_of(i * WIDTH + q * 128, 128), 128)
            xq = x_ref[:, pair]
            gq = g_ref[:, pair]
            xs = jnp.concatenate([xq * left, xq * right], axis=0)
            gs = jnp.concatenate([gq * left, gq * right], axis=0)
            pick = jnp.where(table == head, 1.0, 0.0).astype(BF16)
            v_row = jnp.concatenate([vt[pl.ds(head, 1), :], vt[pl.ds(head + 1, 1), :]], axis=1)
            gate = jnp.exp2(jnp.minimum(mm(apk[...], pick) - v_row, 100.0))
            scores = (gate * cb2).astype(BF16)
            vin[i, :, q * 128 : (q + 1) * 128] = mm(scores, xs)
            turned = jnp.concatenate([scores[:, :tokens].T, scores[:, tokens:].T], axis=1)
            uin[i, :, q * 128 : (q + 1) * 128] = mm(turned, gs)
            d_gate = mm_nt(gq, xs) * gate
            dcb[...] += d_gate[:, :tokens] + d_gate[:, tokens:]

    def forward(i):
        x_i = x_ref[:, cols(i)].astype(F32)
        v = vin[i] + ee[i] * mm(c16, car[i])
        out_ref[:, cols(i)] = (v + ms[i, 0:1, :] * x_i).astype(BF16)
        rowa[...] += to_heads(g_ref[:, cols(i)].astype(F32) * v, i)
        gca[...] += mm_nt(eg[i], car[i])

    def backward(i):
        g_i = g_ref[:, cols(i)].astype(F32)
        u = uin[i]
        from_state = mm(b16, ds[i])
        gx_ref[:, cols(i)] = (u + we[i] * from_state + ms[i, 0:1, :] * g_i).astype(BF16)
        share = x_ref[:, cols(i)].astype(F32) * u + wx[i].astype(F32) * from_state
        cola[...] += to_heads(share, i)
        gba[...] += mm_nt(wx[i], ds[i])

    def sums(i):
        onward = ms[i, 1:2, :] * car[i].astype(F32) + sl[i]
        d_last = jnp.sum(onward * ds[i].astype(F32), axis=0, keepdims=True)
        d_skip = jnp.sum(
            g_ref[:, cols(i)].astype(F32) * x_ref[:, cols(i)].astype(F32), axis=0, keepdims=True)
        row = iota((8, WIDTH), 0)
        both = jnp.where(row == 0, d_last, 0.0) + jnp.where(row == 1, d_skip, 0.0)
        misc[...] += to_heads(both, i)

    def advance(j, _):
        f = j - LAG * jnp.maximum(z - 1, 0)
        b = j - LAG * jnp.maximum(n - 2 - z, 0)
        both = jnp.minimum(f, b)
        f_on = (f >= 0) & (f < chunks)
        b_on = (b >= 0) & (b < chunks)

        @pl.when(f_on & (z > 0))
        def _():
            fcopy(f).wait_recv()
            fsend[f] = (ms[f, 1:2, :] * car[f].astype(F32) + sl[f]).astype(BF16)

        @pl.when(f_on & (z > 0) & (z < n - 1))
        def _():
            fcopy(f).start()

        @pl.when(b_on & (z < n - 1))
        def _():
            bcopy(b).wait_recv()

        @pl.when(b_on & (z < n - 1) & (z > 0))
        def _():
            bsend[b] = (ms[b, 1:2, :] * ds[b].astype(F32) + dc[b]).astype(BF16)
            bcopy(b).start()

        @pl.when(j < chunks)
        def _():
            within(j)

        @pl.when(f_on)
        def _():
            forward(f)

        @pl.when(b_on)
        def _():
            backward(b)

        @pl.when((both >= 0) & (both < chunks))
        def _():
            sums(both)

        return 0

    lax.fori_loop(0, chunks + LAG * max(n - 2, 0), advance, 0)

    d_cum = rowa[...] - cola[...]
    d_cum = d_cum + jnp.where(iota(square, 0) == tokens - 1, misc[0:1, :], 0.0)
    later = iota(square, 0) <= iota(square, 1)
    d_decay = exact(jnp.where(later, 1.0, 0.0), d_cum)
    d_step = cola[...] / step - rate * d_decay
    d_raw = d_step * (1.0 / (1.0 + jnp.exp(-raw)))

    def turn(row, by):
        return pltpu.roll(jnp.broadcast_to(row, (8, tokens)), by, 1)[0:1, :]

    def per_head(row):
        return jnp.where(head_row, row, 0.0)

    mine = (
        per_head(jnp.sum(d_decay * decay, axis=0, keepdims=True))
        + turn(per_head(jnp.sum(d_raw, axis=0, keepdims=True)), heads)
        + turn(per_head(misc[1:2, :]), 2 * heads)
    )

    def seq_copy(d):
        return pltpu.make_async_remote_copy(
            src_ref=reds.at[z], dst_ref=reds.at[z], send_sem=rs_send.at[d - 1],
            recv_sem=rs_recv.at[d - 1], device_id={"seq": lax.rem(z + d, n)},
            device_id_type=pl.DeviceIdType.MESH)

    def batch_copy(d):
        return pltpu.make_async_remote_copy(
            src_ref=redb.at[w], dst_ref=redb.at[w], send_sem=rb_send.at[d - 1],
            recv_sem=rb_recv.at[d - 1], device_id={"batch": lax.rem(w + d, m)},
            device_id_type=pl.DeviceIdType.MESH)

    def flat_copy(d):
        place = z * m + w
        return pltpu.make_async_remote_copy(
            src_ref=redb.at[place], dst_ref=redb.at[place], send_sem=rb_send.at[d - 1],
            recv_sem=rb_recv.at[d - 1], device_id=other(d),
            device_id_type=pl.DeviceIdType.MESH)

    def start(copy):
        return lambda d, _: (copy(d).start(), 0)[1]

    def finish(copy):
        return lambda d, _: (copy(d).wait(), 0)[1]

    if flat:
        redb[z * m + w] = mine
        lax.fori_loop(1, n * m, start(flat_copy), 0)
    else:
        reds[z] = mine
        lax.fori_loop(1, n, start(seq_copy), 0)
    gdt_ref[...] = d_raw.T[0:heads, :]
    d_cb = jnp.where(causal, dcb[...], 0.0)
    gc_ref[...] = (gca[...] + mm(d_cb.astype(BF16), b16)).astype(BF16)
    gb_ref[...] = (gba[...] + mm(d_cb.T.astype(BF16), c16)).astype(BF16)
    if not flat:
        lax.fori_loop(1, n, finish(seq_copy), 0)
        redb[w] = lax.fori_loop(0, n, lambda i, t: t + reds[i], jnp.zeros((1, tokens), F32))
        lax.fori_loop(1, m, start(batch_copy), 0)

    def drain(i, _):
        @pl.when(z < n - 1)
        def _():
            fcopy(i).wait_send()

        @pl.when(z > 0)
        def _():
            bcopy(i).wait_send()

        return 0

    lax.fori_loop(0, chunks, drain, 0)
    if flat:
        lax.fori_loop(1, n * m, finish(flat_copy), 0)
    else:
        lax.fori_loop(1, m, finish(batch_copy), 0)
    total = jnp.sum(redb[...], axis=0)
    ga_out[...] = total[:, :heads]
    gbias_out[...] = turn(total, tokens - heads)[:, :heads]
    gskip_out[...] = turn(total, tokens - 2 * heads)[:, :heads]


def place_outputs(count, *refs):
    sems = refs[2 * count]
    copies = [
        pltpu.make_async_copy(refs[i], refs[count + i], sems.at[i]) for i in range(count)
    ]
    for copy in copies:
        copy.start()
    for copy in copies:
        copy.wait()


def shards(dt_raw, dt_bias, a_log, d_skip, x_in, b_in, c_in, cotangent):
    n, m = lax.axis_size("seq"), lax.axis_size("batch")
    _, tokens, heads = dt_raw.shape
    channels = x_in.shape[2]
    state = b_in.shape[2]
    chunks = channels // WIDTH
    steps = n * m - 1 if n * m <= FLAT else m - 1
    big = (chunks, tokens, WIDTH)
    square = (tokens, tokens)
    vmem = pl.BlockSpec(memory_space=pltpu.VMEM)
    hbm = pl.BlockSpec(memory_space=pltpu.HBM)
    dma = pltpu.SemaphoreType.DMA
    shape = jax.ShapeDtypeStruct
    made = pl.pallas_call(
        functools.partial(kernel, n, m, heads, tokens),
        out_shape=(
            shape((tokens, channels), BF16),
            shape((tokens, channels), BF16),
            shape((tokens, state), BF16),
            shape((tokens, state), BF16),
            shape((heads, tokens), F32),
        ) + (shape((1, heads), F32),) * 3,
        in_specs=[hbm] * 8,
        out_specs=(vmem,) * 8,
        scratch_shapes=[
            pltpu.VMEM((heads, tokens), F32),
            pltpu.VMEM((1, heads), F32),
            pltpu.VMEM((1, heads), F32),
            pltpu.VMEM((1, heads), F32),
            pltpu.VMEM((tokens, channels), BF16),
            pltpu.VMEM((tokens, state), BF16),
            pltpu.VMEM((tokens, state), BF16),
            pltpu.VMEM((tokens, channels), BF16),
            dma((8,)),
            pltpu.VMEM(square, F32),
            pltpu.VMEM((8, tokens), F32),
            pltpu.VMEM((2 * tokens + 16, tokens), BF16),
            pltpu.VMEM(square, BF16),
            pltpu.VMEM(square, F32),
            pltpu.VMEM((tokens, WIDTH), jnp.int32),
            pltpu.VMEM(square, F32),
            pltpu.VMEM((chunks, 8, WIDTH), F32),
            pltpu.VMEM(big, F32),
            pltpu.VMEM(big, F32),
            pltpu.VMEM(big, BF16),
            pltpu.VMEM(big, BF16),
            pltpu.VMEM(big, F32),
            pltpu.VMEM(big, F32),
            pltpu.VMEM(big, F32),
            pltpu.VMEM(big, F32),
            pltpu.VMEM(big, BF16),
            pltpu.VMEM(big, BF16),
            pltpu.VMEM(big, BF16),
            pltpu.VMEM(big, BF16),
            pltpu.VMEM(square, F32),
            pltpu.VMEM(square, F32),
            pltpu.VMEM((8, tokens), F32),
            pltpu.VMEM(square, F32),
            pltpu.VMEM(square, F32),
            pltpu.VMEM(square, F32),
            pltpu.VMEM((n, 1, tokens), F32),
            pltpu.VMEM((steps + 1, 1, tokens), F32),
            dma((chunks,)), dma((chunks,)), dma((chunks,)), dma((chunks,)),
            dma((n - 1,)), dma((n - 1,)), dma((steps,)), dma((steps,)),
        ],
        compiler_params=pltpu.CompilerParams(
            collective_id=0, has_side_effects=True, vmem_limit_bytes=40 * 2**20),
    )(
        *(pltpu.with_memory_space_constraint(a, pltpu.HBM) for a in (
            dt_raw[0].T, dt_bias[None], a_log[None], d_skip[None],
            x_in[0], b_in[0], c_in[0], cotangent[0]))
    )
    out, gx, gb, gc, gdt, alog, bias, skip = pl.pallas_call(
        functools.partial(place_outputs, 8),
        out_shape=tuple(shape(a.shape, a.dtype) for a in made),
        in_specs=[vmem] * 8,
        out_specs=(hbm,) * 8,
        scratch_shapes=[dma((8,))],
        compiler_params=pltpu.CompilerParams(vmem_limit_bytes=4 * 2**20),
    )(*made)
    return (out[None], gx[None], gb[None], gc[None], gdt.T[None], alog[0], bias[0], skip[0])


def solution(mesh):
    rows = P("batch", "seq", None)
    return jax.shard_map(
        shards,
        mesh=mesh,
        in_specs=(rows, P(), P(), P(), rows, rows, rows, rows),
        out_specs=(rows, rows, rows, rows, rows, P(), P(), P()),
        check_vma=False,
    )
```

```python
import functools

import jax
import jax.numpy as jnp
from jax import lax
from jax.experimental import pallas as pl
from jax.experimental.pallas import tpu as pltpu
from jax.sharding import PartitionSpec as P

HEAD_DIM = 64
WIDTH = 256
LAG = 3
UNROLL = 2
FLAT = 64
LOG2E = 1.4426950408889634
F32 = jnp.float32
BF16 = jnp.bfloat16


def mm(a, b):
    return jnp.dot(a, b, preferred_element_type=F32)


def mm_nt(a, b):
    return lax.dot_general(a, b, (((1,), (1,)), ((), ())), preferred_element_type=F32)


def exact(a, b):
    return jnp.dot(a, b, preferred_element_type=F32, precision=lax.Precision.HIGHEST)


def iota(shape, dim):
    return lax.broadcasted_iota(jnp.int32, shape, dim)


def split3(value, heads):
    high = value.astype(BF16).astype(F32)
    rest = value - high
    mid = rest.astype(BF16).astype(F32)
    low = (rest - mid).astype(BF16).astype(F32)
    packed = high + pltpu.roll(mid, heads, 1) + pltpu.roll(low, 2 * heads, 1)
    return packed.astype(BF16)


def kernel(
    n, m, heads, tokens,
    dt_hbm, bias_hbm, alog_hbm, skip_hbm, x_hbm, b_hbm, c_hbm, g_hbm,
    out_ref, gx_ref, gb_ref, gc_ref, gdt_ref, ga_out, gbias_out, gskip_out,
    dt_ref, bias_ref, alog_ref, skip_ref, x_ref, b_ref, c_ref, g_ref,
    in_sem, pad, prm, pk, apk, vt, kmod, cbm, ms, ee, we, wx, eg, sl, dc, vin, uin,
    fsend, car, bsend, ds,
    cum_ref, ratio, slow, rowa, cola, misc, dcb, gba, gca, reds, redb,
    fs_sem, fr_sem, bs_sem, br_sem, rs_send, rs_recv, rb_send, rb_recv,
):
    z = lax.axis_index("seq")
    w = lax.axis_index("batch")
    chunks = heads * HEAD_DIM // WIDTH
    per = WIDTH // HEAD_DIM

    fetches = [
        pltpu.make_async_copy(a, b, in_sem.at[i])
        for i, (a, b) in enumerate((
            (dt_hbm, dt_ref), (bias_hbm, bias_ref), (alog_hbm, alog_ref), (skip_hbm, skip_ref),
            (b_hbm, b_ref), (c_hbm, c_ref), (x_hbm, x_ref), (g_hbm, g_ref)))
    ]
    for fetch in fetches:
        fetch.start()
    barrier = pltpu.get_barrier_semaphore()

    def wrap(place, size):
        return jnp.where(place >= size, place - size, place)

    ring_z = [wrap(z + d, n) for d in range(n)]
    ring_w = [wrap(w + d, m) for d in range(m)]

    def other(d):
        return {"seq": ring_z[d // m], "batch": ring_w[d % m]}

    def greet_seq(d, _):
        pl.semaphore_signal(barrier, inc=1, device_id={"seq": lax.rem(z + d, n)},
                            device_id_type=pl.DeviceIdType.MESH)
        return 0

    def greet_batch(d, _):
        pl.semaphore_signal(barrier, inc=1, device_id={"batch": lax.rem(w + d, m)},
                            device_id_type=pl.DeviceIdType.MESH)
        return 0

    flat = n * m <= FLAT
    peers = n * m - 1 if flat else n + m - 2
    if flat:
        for d in range(1, n * m):
            pl.semaphore_signal(barrier, inc=1, device_id=other(d),
                                device_id_type=pl.DeviceIdType.MESH)
    else:
        lax.fori_loop(1, n, greet_seq, 0)
        lax.fori_loop(1, m, greet_batch, 0)

    def fcopy(i):
        return pltpu.make_async_remote_copy(
            src_ref=fsend.at[i], dst_ref=car.at[i], send_sem=fs_sem.at[i], recv_sem=fr_sem.at[i],
            device_id={"seq": jnp.minimum(z + 1, n - 1)}, device_id_type=pl.DeviceIdType.MESH)

    def bcopy(i):
        return pltpu.make_async_remote_copy(
            src_ref=bsend.at[i], dst_ref=ds.at[i], send_sem=bs_sem.at[i], recv_sem=br_sem.at[i],
            device_id={"seq": jnp.maximum(z - 1, 0)}, device_id_type=pl.DeviceIdType.MESH)

    pad[...] = jnp.zeros_like(pad)
    prm[...] = jnp.zeros_like(prm)
    for fetch in fetches[:6]:
        fetch.wait()
    pad[0:heads, :] = dt_ref[...]
    prm[0:1, :heads] = bias_ref[...]
    prm[1:2, :heads] = alog_ref[...]
    prm[2:3, :heads] = skip_ref[...]
    square = (tokens, tokens)
    is_head = iota(square, 1) < heads
    raw = pad[...].T + prm[0:1, :]
    step = jnp.maximum(raw, 0.0) + jnp.log1p(jnp.exp(-jnp.abs(raw)))
    rate = jnp.exp(prm[1:2, :])
    decay = jnp.where(is_head, -rate * step, 0.0)
    causal = iota(square, 0) >= iota(square, 1)
    slope = 1.0 / (1.0 + jnp.exp(-raw))
    both_sums = exact(jnp.where(causal, 1.0, 0.0), jnp.concatenate([decay, slope], axis=1))
    cum = both_sums[:, :tokens]
    cum_ref[...] = cum
    ratio[...] = slope / step
    slow[...] = rate * both_sums[:, tokens:]
    last = cum[tokens - 1 : tokens, :]
    pk[0:tokens, :] = split3(jnp.where(is_head, jnp.exp(cum), 0.0), heads)
    pk[tokens : 2 * tokens, :] = split3(
        jnp.where(is_head, jnp.exp(last - cum) * step, 0.0), heads)
    head_row = is_head[0:1, :]
    factor = jnp.where(head_row, jnp.exp(last.astype(BF16).astype(F32)), 0.0)
    row16 = iota((16, tokens), 0)
    pk[2 * tokens : 2 * tokens + 16, :] = split3(
        jnp.where(row16 == 0, prm[2:3, :], 0.0) + jnp.where(row16 == 1, factor, 0.0), heads)
    k = iota((tokens, WIDTH), 0)
    kmod[...] = k - jnp.where(k >= heads, heads, 0) - jnp.where(k >= 2 * heads, heads, 0)
    b16 = b_ref[...]
    c16 = c_ref[...]
    bt = b16.astype(F32).T.astype(BF16)
    ct = c16.astype(F32).T.astype(BF16)

    for fetch in fetches[6:]:
        fetch.wait()
    edge = (z == 0) | (z == n - 1)

    def cols(i):
        return pl.ds(pl.multiple_of(i * WIDTH, WIDTH), WIDTH)

    def state(i):
        group = lax.shift_right_logical(iota((tokens, WIDTH), 1), 6)
        spread = jnp.where(kmod[...] - group == i * per, 1.0, 0.0).astype(BF16)
        wide = mm(pk[...], spread)
        ee[i] = wide[0:tokens]
        we[i] = wide[tokens : 2 * tokens]
        ms[i] = wide[2 * tokens : 2 * tokens + 8]
        wx_i = (x_ref[:, cols(i)].astype(F32) * wide[tokens : 2 * tokens]).astype(BF16)
        eg_i = (g_ref[:, cols(i)].astype(F32) * wide[0:tokens]).astype(BF16)
        wx[i] = wx_i
        eg[i] = eg_i
        sl[i] = mm(bt, wx_i)
        dc[i] = mm(ct, eg_i)

    def states(k, _):
        for u in range(UNROLL):
            state(k * UNROLL + u)

        @pl.when((k == 0) & edge)
        def _():
            pl.semaphore_wait(barrier, peers)

        for u in range(UNROLL):
            i = k * UNROLL + u

            @pl.when(z == 0)
            def _():
                car[i] = jnp.zeros((tokens, WIDTH), BF16)
                fsend[i] = sl[i].astype(BF16)
                fcopy(i).start()

            @pl.when(z == n - 1)
            def _():
                ds[i] = jnp.zeros((tokens, WIDTH), BF16)
                bsend[i] = dc[i].astype(BF16)
                bcopy(i).start()

        return 0

    lax.fori_loop(0, chunks // UNROLL, states, 0)

    cum2 = cum * LOG2E
    apk[...] = split3(cum2, heads)
    vt[...] = (cum2 - jnp.log(step) * LOG2E).T
    cbm[...] = jnp.where(causal, mm(c16, bt), 0.0)
    for acc in (rowa, cola, misc, dcb, gba, gca):
        acc[...] = jnp.zeros_like(acc)

    @pl.when(jnp.logical_not(edge))
    def _():
        pl.semaphore_wait(barrier, peers)


    def to_heads(value, i):
        group = lax.shift_right_logical(iota((WIDTH, tokens), 0), 6)
        gather = jnp.where(iota((WIDTH, tokens), 1) - group == i * per, 1.0, 0.0).astype(BF16)
        high = value.astype(BF16)
        low = (value - high.astype(F32)).astype(BF16)
        return mm(high, gather) + mm(low, gather)

    def within(i):
        lane = iota(square, 1)
        left = jnp.where(lane < HEAD_DIM, 1.0, 0.0).astype(BF16)
        right = jnp.where(lane < HEAD_DIM, 0.0, 1.0).astype(BF16)
        second = jnp.where(iota((tokens, 2 * tokens), 1) < tokens, 0, 1)
        table = kmod[:, 0:1] - second
        cb2 = jnp.concatenate([cbm[...], cbm[...]], axis=1)
        for q in range(WIDTH // 128):
            head = i * per + 2 * q
            pair = pl.ds(pl.multiple_of(i * WIDTH + q * 128, 128), 128)
            xq = x_ref[:, pair]
            gq = g_ref[:, pair]
            xs = jnp.concatenate([xq * left, xq * right], axis=0)
            gs = jnp.concatenate([gq * left, gq * right], axis=0)
            pick = jnp.where(table == head, 1.0, 0.0).astype(BF16)
            v_row = jnp.concatenate([vt[pl.ds(head, 1), :], vt[pl.ds(head + 1, 1), :]], axis=1)
            gate = jnp.exp2(jnp.minimum(mm(apk[...], pick) - v_row, 100.0))
            scores = (gate * cb2).astype(BF16)
            vin[i, :, q * 128 : (q + 1) * 128] = mm(scores, xs)
            turned = jnp.concatenate([scores[:, :tokens].T, scores[:, tokens:].T], axis=1)
            uin[i, :, q * 128 : (q + 1) * 128] = mm(turned, gs)
            d_gate = mm_nt(gq, xs) * gate
            dcb[...] += d_gate[:, :tokens] + d_gate[:, tokens:]

    def forward(i):
        x_i = x_ref[:, cols(i)].astype(F32)
        v = vin[i] + ee[i] * mm(c16, car[i])
        out_ref[:, cols(i)] = (v + ms[i, 0:1, :] * x_i).astype(BF16)
        rowa[...] += to_heads(g_ref[:, cols(i)].astype(F32) * v, i)
        gca[...] += mm_nt(eg[i], car[i])

    def backward(i):
        g_i = g_ref[:, cols(i)].astype(F32)
        u = uin[i]
        from_state = mm(b16, ds[i])
        gx_ref[:, cols(i)] = (u + we[i] * from_state + ms[i, 0:1, :] * g_i).astype(BF16)
        share = x_ref[:, cols(i)].astype(F32) * u + wx[i].astype(F32) * from_state
        cola[...] += to_heads(share, i)
        gba[...] += mm_nt(wx[i], ds[i])

    def sums(i):
        onward = ms[i, 1:2, :] * car[i].astype(F32) + sl[i]
        d_last = jnp.sum(onward * ds[i].astype(F32), axis=0, keepdims=True)
        d_skip = jnp.sum(
            g_ref[:, cols(i)].astype(F32) * x_ref[:, cols(i)].astype(F32), axis=0, keepdims=True)
        row = iota((8, WIDTH), 0)
        both = jnp.where(row == 0, d_last, 0.0) + jnp.where(row == 1, d_skip, 0.0)
        misc[...] += to_heads(both, i)

    cases = set()
    for place in range(n):
        for j in range(chunks + LAG * max(n - 2, 0)):
            f = j - LAG * max(place - 1, 0)
            b = j - LAG * max(n - 2 - place, 0)
            marks = (j < chunks, 0 <= f < chunks, 0 <= b < chunks, 0 <= min(f, b) < chunks)
            cases.add(sum(1 << k for k, mark in enumerate(marks) if mark))
    cases = sorted(cases - {0})

    def advance(j, _):
        f = j - LAG * jnp.maximum(z - 1, 0)
        b = j - LAG * jnp.maximum(n - 2 - z, 0)
        both = jnp.minimum(f, b)
        f_on = (f >= 0) & (f < chunks)
        b_on = (b >= 0) & (b < chunks)

        @pl.when(f_on & (z > 0))
        def _():
            fcopy(f).wait_recv()
            fsend[f] = (ms[f, 1:2, :] * car[f].astype(F32) + sl[f]).astype(BF16)

        @pl.when(f_on & (z > 0) & (z < n - 1))
        def _():
            fcopy(f).start()

        @pl.when(b_on & (z < n - 1))
        def _():
            bcopy(b).wait_recv()

        @pl.when(b_on & (z < n - 1) & (z > 0))
        def _():
            bsend[b] = (ms[b, 1:2, :] * ds[b].astype(F32) + dc[b]).astype(BF16)
            bcopy(b).start()

        kind = (
            jnp.where(j < chunks, 1, 0) + jnp.where(f_on, 2, 0) + jnp.where(b_on, 4, 0)
            + jnp.where((both >= 0) & (both < chunks), 8, 0)
        )
        for case in cases:

            @pl.when(kind == case)
            def _():
                if case & 1:
                    within(j)
                if case & 2:
                    forward(f)
                if case & 4:
                    backward(b)
                if case & 8:
                    sums(both)

        return 0

    lax.fori_loop(0, chunks + LAG * max(n - 2, 0), advance, 0)

    d_cum = rowa[...] - cola[...]
    d_cum = d_cum + jnp.where(iota(square, 0) == tokens - 1, misc[0:1, :], 0.0)
    grad_a = jnp.sum(d_cum * cum_ref[...], axis=0, keepdims=True)
    grad_bias = jnp.sum(cola[...] * ratio[...] - d_cum * slow[...], axis=0, keepdims=True)

    def turn(row, by):
        return pltpu.roll(jnp.broadcast_to(row, (8, tokens)), by, 1)[0:1, :]

    def per_head(row):
        return jnp.where(head_row, row, 0.0)

    mine = (
        per_head(grad_a) + turn(per_head(grad_bias), heads)
        + turn(per_head(misc[1:2, :]), 2 * heads)
    )

    def seq_copy(d):
        return pltpu.make_async_remote_copy(
            src_ref=reds.at[z], dst_ref=reds.at[z], send_sem=rs_send.at[d - 1],
            recv_sem=rs_recv.at[d - 1], device_id={"seq": lax.rem(z + d, n)},
            device_id_type=pl.DeviceIdType.MESH)

    def batch_copy(d):
        return pltpu.make_async_remote_copy(
            src_ref=redb.at[w], dst_ref=redb.at[w], send_sem=rb_send.at[d - 1],
            recv_sem=rb_recv.at[d - 1], device_id={"batch": lax.rem(w + d, m)},
            device_id_type=pl.DeviceIdType.MESH)

    def flat_copy(d):
        place = z * m + w
        return pltpu.make_async_remote_copy(
            src_ref=redb.at[place], dst_ref=redb.at[place], send_sem=rb_send.at[d - 1],
            recv_sem=rb_recv.at[d - 1], device_id=other(d),
            device_id_type=pl.DeviceIdType.MESH)

    def start(copy):
        return lambda d, _: (copy(d).start(), 0)[1]

    def finish(copy):
        return lambda d, _: (copy(d).wait(), 0)[1]

    if flat:
        redb[z * m + w] = mine
        for d in range(1, n * m):
            flat_copy(d).start()
    else:
        reds[z] = mine
        lax.fori_loop(1, n, start(seq_copy), 0)
    later = iota(square, 0) <= iota(square, 1)
    d_decay = exact(jnp.where(later, 1.0, 0.0), d_cum)
    d_raw = cola[...] * ratio[...] - rate * slope * d_decay
    gdt_ref[...] = d_raw.T[0:heads, :]
    d_cb = jnp.where(causal, dcb[...], 0.0)
    gc_ref[...] = (gca[...] + mm(d_cb.astype(BF16), b16)).astype(BF16)
    gb_ref[...] = (gba[...] + mm(d_cb.T.astype(BF16), c16)).astype(BF16)
    if not flat:
        lax.fori_loop(1, n, finish(seq_copy), 0)
        redb[w] = lax.fori_loop(0, n, lambda i, t: t + reds[i], jnp.zeros((1, tokens), F32))
        lax.fori_loop(1, m, start(batch_copy), 0)

    def drain(i, _):
        @pl.when(z < n - 1)
        def _():
            fcopy(i).wait_send()

        @pl.when(z > 0)
        def _():
            bcopy(i).wait_send()

        return 0

    lax.fori_loop(0, chunks, drain, 0)
    if flat:
        for d in range(1, n * m):
            flat_copy(d).wait()
    else:
        lax.fori_loop(1, m, finish(batch_copy), 0)
    total = jnp.sum(redb[...], axis=0)
    ga_out[...] = total[:, :heads]
    gbias_out[...] = turn(total, tokens - heads)[:, :heads]
    gskip_out[...] = turn(total, tokens - 2 * heads)[:, :heads]


def place_outputs(count, *refs):
    sems = refs[2 * count]
    copies = [
        pltpu.make_async_copy(refs[i], refs[count + i], sems.at[i]) for i in range(count)
    ]
    for copy in copies:
        copy.start()
    for copy in copies:
        copy.wait()


def shards(dt_raw, dt_bias, a_log, d_skip, x_in, b_in, c_in, cotangent):
    n, m = lax.axis_size("seq"), lax.axis_size("batch")
    _, tokens, heads = dt_raw.shape
    channels = x_in.shape[2]
    state = b_in.shape[2]
    chunks = channels // WIDTH
    steps = n * m - 1 if n * m <= FLAT else m - 1
    big = (chunks, tokens, WIDTH)
    square = (tokens, tokens)
    vmem = pl.BlockSpec(memory_space=pltpu.VMEM)
    hbm = pl.BlockSpec(memory_space=pltpu.HBM)
    dma = pltpu.SemaphoreType.DMA
    shape = jax.ShapeDtypeStruct
    made = pl.pallas_call(
        functools.partial(kernel, n, m, heads, tokens),
        out_shape=(
            shape((tokens, channels), BF16),
            shape((tokens, channels), BF16),
            shape((tokens, state), BF16),
            shape((tokens, state), BF16),
            shape((heads, tokens), F32),
        ) + (shape((1, heads), F32),) * 3,
        in_specs=[hbm] * 8,
        out_specs=(vmem,) * 8,
        scratch_shapes=[
            pltpu.VMEM((heads, tokens), F32),
            pltpu.VMEM((1, heads), F32),
            pltpu.VMEM((1, heads), F32),
            pltpu.VMEM((1, heads), F32),
            pltpu.VMEM((tokens, channels), BF16),
            pltpu.VMEM((tokens, state), BF16),
            pltpu.VMEM((tokens, state), BF16),
            pltpu.VMEM((tokens, channels), BF16),
            dma((8,)),
            pltpu.VMEM(square, F32),
            pltpu.VMEM((8, tokens), F32),
            pltpu.VMEM((2 * tokens + 16, tokens), BF16),
            pltpu.VMEM(square, BF16),
            pltpu.VMEM(square, F32),
            pltpu.VMEM((tokens, WIDTH), jnp.int32),
            pltpu.VMEM(square, F32),
            pltpu.VMEM((chunks, 8, WIDTH), F32),
            pltpu.VMEM(big, F32),
            pltpu.VMEM(big, F32),
            pltpu.VMEM(big, BF16),
            pltpu.VMEM(big, BF16),
            pltpu.VMEM(big, F32),
            pltpu.VMEM(big, F32),
            pltpu.VMEM(big, F32),
            pltpu.VMEM(big, F32),
            pltpu.VMEM(big, BF16),
            pltpu.VMEM(big, BF16),
            pltpu.VMEM(big, BF16),
            pltpu.VMEM(big, BF16),
            pltpu.VMEM(square, F32),
            pltpu.VMEM(square, F32),
            pltpu.VMEM(square, F32),
            pltpu.VMEM(square, F32),
            pltpu.VMEM(square, F32),
            pltpu.VMEM((8, tokens), F32),
            pltpu.VMEM(square, F32),
            pltpu.VMEM(square, F32),
            pltpu.VMEM(square, F32),
            pltpu.VMEM((n, 1, tokens), F32),
            pltpu.VMEM((steps + 1, 1, tokens), F32),
            dma((chunks,)), dma((chunks,)), dma((chunks,)), dma((chunks,)),
            dma((n - 1,)), dma((n - 1,)), dma((steps,)), dma((steps,)),
        ],
        compiler_params=pltpu.CompilerParams(
            collective_id=0, has_side_effects=True, vmem_limit_bytes=40 * 2**20),
    )(
        *(pltpu.with_memory_space_constraint(a, pltpu.HBM) for a in (
            dt_raw[0].T, dt_bias[None], a_log[None], d_skip[None],
            x_in[0], b_in[0], c_in[0], cotangent[0]))
    )
    out, gx, gb, gc, gdt, alog, bias, skip = pl.pallas_call(
        functools.partial(place_outputs, 8),
        out_shape=tuple(shape(a.shape, a.dtype) for a in made),
        in_specs=[vmem] * 8,
        out_specs=(hbm,) * 8,
        scratch_shapes=[dma((8,))],
        compiler_params=pltpu.CompilerParams(vmem_limit_bytes=4 * 2**20),
    )(*made)
    return (out[None], gx[None], gb[None], gc[None], gdt.T[None], alog[0], bias[0], skip[0])


def solution(mesh):
    rows = P("batch", "seq", None)
    return jax.shard_map(
        shards,
        mesh=mesh,
        in_specs=(rows, P(), P(), P(), rows, rows, rows, rows),
        out_specs=(rows, rows, rows, rows, rows, P(), P(), P()),
        check_vma=False,
    )
```

```python
import functools

import jax
import jax.numpy as jnp
from jax import lax
from jax.experimental import pallas as pl
from jax.experimental.pallas import tpu as pltpu
from jax.sharding import PartitionSpec as P

HEAD_DIM = 64
WIDTH = 256
F_LAG = 2
B_LAG = 3
UNROLL = 3
FLAT = 64
LOG2E = 1.4426950408889634
F32 = jnp.float32
BF16 = jnp.bfloat16


def mm(a, b):
    return jnp.dot(a, b, preferred_element_type=F32)


def mm_nt(a, b):
    return lax.dot_general(a, b, (((1,), (1,)), ((), ())), preferred_element_type=F32)


def exact(a, b):
    return jnp.dot(a, b, preferred_element_type=F32, precision=lax.Precision.HIGHEST)


def iota(shape, dim):
    return lax.broadcasted_iota(jnp.int32, shape, dim)


def split3(value, heads):
    high = value.astype(BF16).astype(F32)
    rest = value - high
    mid = rest.astype(BF16).astype(F32)
    low = (rest - mid).astype(BF16).astype(F32)
    packed = high + pltpu.roll(mid, heads, 1) + pltpu.roll(low, 2 * heads, 1)
    return packed.astype(BF16)


def kernel(
    n, m, heads, tokens,
    dt_hbm, bias_hbm, alog_hbm, skip_hbm, x_hbm, b_hbm, c_hbm, g_hbm,
    out_ref, gx_ref, gb_ref, gc_ref, gdt_ref, ga_out, gbias_out, gskip_out,
    dt_ref, bias_ref, alog_ref, skip_ref, x_ref, b_ref, c_ref, g_ref,
    in_sem, pad, prm, pk, apk, vt, kmod, cbm, ms, ee, we, wx, eg, sl, dc, vin, uin,
    fsend, car, bsend, ds,
    cum_ref, ratio, slow, rowa, cola, misc, dcb, gba, gca, reds, redb,
    fs_sem, fr_sem, bs_sem, br_sem, rs_send, rs_recv, rb_send, rb_recv,
):
    z = lax.axis_index("seq")
    w = lax.axis_index("batch")
    chunks = heads * HEAD_DIM // WIDTH
    per = WIDTH // HEAD_DIM

    fetches = [
        pltpu.make_async_copy(a, b, in_sem.at[i])
        for i, (a, b) in enumerate((
            (dt_hbm, dt_ref), (bias_hbm, bias_ref), (alog_hbm, alog_ref), (skip_hbm, skip_ref),
            (b_hbm, b_ref), (c_hbm, c_ref), (x_hbm, x_ref), (g_hbm, g_ref)))
    ]
    for fetch in fetches:
        fetch.start()
    barrier = pltpu.get_barrier_semaphore()

    def wrap(place, size):
        return jnp.where(place >= size, place - size, place)

    ring_z = [wrap(z + d, n) for d in range(n)]
    ring_w = [wrap(w + d, m) for d in range(m)]

    def other(d):
        return {"seq": ring_z[d // m], "batch": ring_w[d % m]}

    def greet_seq(d, _):
        pl.semaphore_signal(barrier, inc=1, device_id={"seq": lax.rem(z + d, n)},
                            device_id_type=pl.DeviceIdType.MESH)
        return 0

    def greet_batch(d, _):
        pl.semaphore_signal(barrier, inc=1, device_id={"batch": lax.rem(w + d, m)},
                            device_id_type=pl.DeviceIdType.MESH)
        return 0

    flat = n * m <= FLAT
    relay = flat and n > 3
    peers = n * m - 1 if flat else n + m - 2
    edge_peers = 1 if relay else peers
    if relay:
        @pl.when((z == 1) | (z == n - 2))
        def _():
            pl.semaphore_signal(
                barrier, inc=1, device_id={"seq": jnp.where(z == 1, 0, n - 1)},
                device_id_type=pl.DeviceIdType.MESH)

        for dw in range(m):
            for inner in range(1, n - 1):

                def greet():
                    pl.semaphore_signal(
                        barrier, inc=1, device_id={"seq": inner, "batch": ring_w[dw]},
                        device_id_type=pl.DeviceIdType.MESH)

                if dw:
                    greet()
                else:
                    pl.when(z != inner)(greet)
    elif flat:
        for d in range(1, n * m):
            pl.semaphore_signal(barrier, inc=1, device_id=other(d),
                                device_id_type=pl.DeviceIdType.MESH)
    else:
        lax.fori_loop(1, n, greet_seq, 0)
        lax.fori_loop(1, m, greet_batch, 0)

    def fcopy(i):
        return pltpu.make_async_remote_copy(
            src_ref=fsend.at[i], dst_ref=car.at[i], send_sem=fs_sem.at[i], recv_sem=fr_sem.at[i],
            device_id={"seq": jnp.minimum(z + 1, n - 1)}, device_id_type=pl.DeviceIdType.MESH)

    def bcopy(i):
        return pltpu.make_async_remote_copy(
            src_ref=bsend.at[i], dst_ref=ds.at[i], send_sem=bs_sem.at[i], recv_sem=br_sem.at[i],
            device_id={"seq": jnp.maximum(z - 1, 0)}, device_id_type=pl.DeviceIdType.MESH)

    pad[...] = jnp.zeros_like(pad)
    prm[...] = jnp.zeros_like(prm)
    for fetch in fetches[:6]:
        fetch.wait()
    pad[0:heads, :] = dt_ref[...]
    prm[0:1, :heads] = bias_ref[...]
    prm[1:2, :heads] = alog_ref[...]
    prm[2:3, :heads] = skip_ref[...]
    square = (tokens, tokens)
    is_head = iota(square, 1) < heads
    raw = pad[...].T + prm[0:1, :]
    step = jnp.maximum(raw, 0.0) + jnp.log1p(jnp.exp(-jnp.abs(raw)))
    rate = jnp.exp(prm[1:2, :])
    decay = jnp.where(is_head, -rate * step, 0.0)
    causal = iota(square, 0) >= iota(square, 1)
    slope = 1.0 / (1.0 + jnp.exp(-raw))
    cum = exact(jnp.where(causal, 1.0, 0.0), decay)
    last = cum[tokens - 1 : tokens, :]
    pk[0:tokens, :] = split3(jnp.where(is_head, jnp.exp(cum), 0.0), heads)
    pk[tokens : 2 * tokens, :] = split3(
        jnp.where(is_head, jnp.exp(last - cum) * step, 0.0), heads)
    head_row = is_head[0:1, :]
    factor = jnp.where(head_row, jnp.exp(last.astype(BF16).astype(F32)), 0.0)
    row16 = iota((16, tokens), 0)
    pk[2 * tokens : 2 * tokens + 16, :] = split3(
        jnp.where(row16 == 0, prm[2:3, :], 0.0) + jnp.where(row16 == 1, factor, 0.0), heads)
    k = iota((tokens, WIDTH), 0)
    kmod[...] = k - jnp.where(k >= heads, heads, 0) - jnp.where(k >= 2 * heads, heads, 0)
    b16 = b_ref[...]
    c16 = c_ref[...]
    bt = b16.astype(F32).T.astype(BF16)
    ct = c16.astype(F32).T.astype(BF16)

    for fetch in fetches[6:]:
        fetch.wait()
    edge = (z == 0) | (z == n - 1)
    place = z * m + w

    def cols(i):
        return pl.ds(pl.multiple_of(i * WIDTH, WIDTH), WIDTH)

    def state(i):
        group = lax.shift_right_logical(iota((tokens, WIDTH), 1), 6)
        spread = jnp.where(kmod[...] - group == i * per, 1.0, 0.0).astype(BF16)
        wide = mm(pk[...], spread)
        ee[i] = wide[0:tokens]
        we[i] = wide[tokens : 2 * tokens]
        ms[i] = wide[2 * tokens : 2 * tokens + 8]
        wx_i = (x_ref[:, cols(i)].astype(F32) * wide[tokens : 2 * tokens]).astype(BF16)
        eg_i = (g_ref[:, cols(i)].astype(F32) * wide[0:tokens]).astype(BF16)
        wx[i] = wx_i
        eg[i] = eg_i
        sl[i] = mm(bt, wx_i)
        dc[i] = mm(ct, eg_i)

    def announce(i):
        @pl.when(z == 0)
        def _():
            car[i] = jnp.zeros((tokens, WIDTH), BF16)
            fsend[i] = sl[i].astype(BF16)
            fcopy(i).start()

        @pl.when(z == n - 1)
        def _():
            ds[i] = jnp.zeros((tokens, WIDTH), BF16)
            bsend[i] = dc[i].astype(BF16)
            bcopy(i).start()

    def states(k, _):
        for u in range(unroll):
            state(1 + k * unroll + u)
        for u in range(unroll):
            announce(1 + k * unroll + u)
        return 0

    state(0)

    @pl.when(edge)
    def _():
        pl.semaphore_wait(barrier, edge_peers)

    announce(0)
    unroll = UNROLL if (chunks - 1) % UNROLL == 0 else 1
    lax.fori_loop(0, (chunks - 1) // unroll, states, 0)

    cum_ref[...] = cum
    ratio[...] = slope / step
    slow[...] = rate * exact(jnp.where(causal, 1.0, 0.0), slope)
    cum2 = cum * LOG2E
    apk[...] = split3(cum2, heads)
    vt[...] = (cum2 - jnp.log(step) * LOG2E).T
    cbm[...] = jnp.where(causal, mm(c16, bt), 0.0)
    for acc in (rowa, cola, misc, dcb, gba, gca):
        acc[...] = jnp.zeros_like(acc)

    @pl.when(jnp.logical_not(edge))
    def _():
        pl.semaphore_wait(barrier, peers)


    def to_heads(value, i):
        group = lax.shift_right_logical(iota((WIDTH, tokens), 0), 6)
        gather = jnp.where(iota((WIDTH, tokens), 1) - group == i * per, 1.0, 0.0).astype(BF16)
        high = value.astype(BF16)
        low = (value - high.astype(F32)).astype(BF16)
        return mm(high, gather) + mm(low, gather)

    def within(i):
        lane = iota(square, 1)
        left = jnp.where(lane < HEAD_DIM, 1.0, 0.0).astype(BF16)
        right = jnp.where(lane < HEAD_DIM, 0.0, 1.0).astype(BF16)
        second = jnp.where(iota((tokens, 2 * tokens), 1) < tokens, 0, 1)
        table = kmod[:, 0:1] - second
        cb2 = jnp.concatenate([cbm[...], cbm[...]], axis=1)
        for q in range(WIDTH // 128):
            head = i * per + 2 * q
            pair = pl.ds(pl.multiple_of(i * WIDTH + q * 128, 128), 128)
            xq = x_ref[:, pair]
            gq = g_ref[:, pair]
            xs = jnp.concatenate([xq * left, xq * right], axis=0)
            gs = jnp.concatenate([gq * left, gq * right], axis=0)
            pick = jnp.where(table == head, 1.0, 0.0).astype(BF16)
            v_row = jnp.concatenate([vt[pl.ds(head, 1), :], vt[pl.ds(head + 1, 1), :]], axis=1)
            gate = jnp.exp2(jnp.minimum(mm(apk[...], pick) - v_row, 100.0))
            scores = (gate * cb2).astype(BF16)
            vin[i, :, q * 128 : (q + 1) * 128] = mm(scores, xs)
            turned = jnp.concatenate([scores[:, :tokens].T, scores[:, tokens:].T], axis=1)
            uin[i, :, q * 128 : (q + 1) * 128] = mm(turned, gs)
            d_gate = mm_nt(gq, xs) * gate
            dcb[...] += d_gate[:, :tokens] + d_gate[:, tokens:]

    def forward(i):
        x_i = x_ref[:, cols(i)].astype(F32)
        v = vin[i] + ee[i] * mm(c16, car[i])
        out_ref[:, cols(i)] = (v + ms[i, 0:1, :] * x_i).astype(BF16)
        rowa[...] += to_heads(g_ref[:, cols(i)].astype(F32) * v, i)
        gca[...] += mm_nt(eg[i], car[i])

    def backward(i):
        g_i = g_ref[:, cols(i)].astype(F32)
        u = uin[i]
        from_state = mm(b16, ds[i])
        gx_ref[:, cols(i)] = (u + we[i] * from_state + ms[i, 0:1, :] * g_i).astype(BF16)
        share = x_ref[:, cols(i)].astype(F32) * u + wx[i].astype(F32) * from_state
        cola[...] += to_heads(share, i)
        gba[...] += mm_nt(wx[i], ds[i])

    def sums(i):
        onward = ms[i, 1:2, :] * car[i].astype(F32) + sl[i]
        d_last = jnp.sum(onward * ds[i].astype(F32), axis=0, keepdims=True)
        d_skip = jnp.sum(
            g_ref[:, cols(i)].astype(F32) * x_ref[:, cols(i)].astype(F32), axis=0, keepdims=True)
        row = iota((8, WIDTH), 0)
        both = jnp.where(row == 0, d_last, 0.0) + jnp.where(row == 1, d_skip, 0.0)
        misc[...] += to_heads(both, i)

    cases = set()
    for row in range(n):
        for j in range(chunks + max(F_LAG, B_LAG) * max(n - 2, 0)):
            f = j - F_LAG * max(row - 1, 0)
            b = j - B_LAG * max(n - 2 - row, 0)
            marks = (j < chunks, 0 <= f < chunks, 0 <= b < chunks, 0 <= min(f, b) < chunks)
            cases.add(sum(1 << k for k, mark in enumerate(marks) if mark))
    cases = sorted(cases - {0})

    def advance(j, _):
        f = j - F_LAG * jnp.maximum(z - 1, 0)
        b = j - B_LAG * jnp.maximum(n - 2 - z, 0)
        both = jnp.minimum(f, b)
        f_on = (f >= 0) & (f < chunks)
        b_on = (b >= 0) & (b < chunks)

        @pl.when(f_on & (z > 0))
        def _():
            fcopy(f).wait_recv()
            fsend[f] = (ms[f, 1:2, :] * car[f].astype(F32) + sl[f]).astype(BF16)

        @pl.when(f_on & (z > 0) & (z < n - 1))
        def _():
            fcopy(f).start()

        @pl.when(b_on & (z < n - 1))
        def _():
            bcopy(b).wait_recv()

        @pl.when(b_on & (z < n - 1) & (z > 0))
        def _():
            bsend[b] = (ms[b, 1:2, :] * ds[b].astype(F32) + dc[b]).astype(BF16)
            bcopy(b).start()

        kind = (
            jnp.where(j < chunks, 1, 0) + jnp.where(f_on, 2, 0) + jnp.where(b_on, 4, 0)
            + jnp.where((both >= 0) & (both < chunks), 8, 0)
        )
        for case in cases:

            @pl.when(kind == case)
            def _():
                if case & 1:
                    within(j)
                if case & 2:
                    forward(f)
                if case & 4:
                    backward(b)
                if case & 8:
                    sums(both)

        return 0

    lax.fori_loop(0, chunks + max(F_LAG, B_LAG) * max(n - 2, 0), advance, 0)

    d_cum = rowa[...] - cola[...]
    d_cum = d_cum + jnp.where(iota(square, 0) == tokens - 1, misc[0:1, :], 0.0)
    grad_a = jnp.sum(d_cum * cum_ref[...], axis=0, keepdims=True)
    grad_bias = jnp.sum(cola[...] * ratio[...] - d_cum * slow[...], axis=0, keepdims=True)

    def turn(row, by):
        return pltpu.roll(jnp.broadcast_to(row, (8, tokens)), by, 1)[0:1, :]

    def per_head(row):
        return jnp.where(head_row, row, 0.0)

    mine = (
        per_head(grad_a) + turn(per_head(grad_bias), heads)
        + turn(per_head(misc[1:2, :]), 2 * heads)
    )

    def seq_copy(d):
        return pltpu.make_async_remote_copy(
            src_ref=reds.at[z], dst_ref=reds.at[z], send_sem=rs_send.at[d - 1],
            recv_sem=rs_recv.at[d - 1], device_id={"seq": lax.rem(z + d, n)},
            device_id_type=pl.DeviceIdType.MESH)

    def batch_copy(d):
        return pltpu.make_async_remote_copy(
            src_ref=redb.at[w], dst_ref=redb.at[w], send_sem=rb_send.at[d - 1],
            recv_sem=rb_recv.at[d - 1], device_id={"batch": lax.rem(w + d, m)},
            device_id_type=pl.DeviceIdType.MESH)

    def flat_copy(to):
        return pltpu.make_async_remote_copy(
            src_ref=redb.at[place], dst_ref=redb.at[place], send_sem=rb_send.at[to],
            recv_sem=rb_recv.at[place],
            device_id={"seq": jnp.int32(to // m), "batch": jnp.int32(to % m)},
            device_id_type=pl.DeviceIdType.MESH)

    def flat_from(source):
        return pltpu.make_async_remote_copy(
            src_ref=redb.at[source], dst_ref=redb.at[source], send_sem=rb_send.at[source],
            recv_sem=rb_recv.at[source],
            device_id={"seq": jnp.int32(source // m), "batch": jnp.int32(source % m)},
            device_id_type=pl.DeviceIdType.MESH)

    def start(copy):
        return lambda d, _: (copy(d).start(), 0)[1]

    def finish(copy):
        return lambda d, _: (copy(d).wait(), 0)[1]

    if flat:
        redb[place] = mine
        for to in range(n * m):
            pl.when(place != to)(lambda: flat_copy(to).start())
    else:
        reds[z] = mine
        lax.fori_loop(1, n, start(seq_copy), 0)
    later = iota(square, 0) <= iota(square, 1)
    d_decay = exact(jnp.where(later, 1.0, 0.0), d_cum)
    d_raw = cola[...] * ratio[...] - rate * slope * d_decay
    gdt_ref[...] = d_raw.T[0:heads, :]
    d_cb = jnp.where(causal, dcb[...], 0.0)
    gc_ref[...] = (gca[...] + mm(d_cb.astype(BF16), b16)).astype(BF16)
    gb_ref[...] = (gba[...] + mm(d_cb.T.astype(BF16), c16)).astype(BF16)
    if not flat:
        lax.fori_loop(1, n, finish(seq_copy), 0)
        redb[w] = lax.fori_loop(0, n, lambda i, t: t + reds[i], jnp.zeros((1, tokens), F32))
        lax.fori_loop(1, m, start(batch_copy), 0)

    def drain(i, _):
        @pl.when(z < n - 1)
        def _():
            fcopy(i).wait_send()

        @pl.when(z > 0)
        def _():
            bcopy(i).wait_send()

        return 0

    lax.fori_loop(0, chunks, drain, 0)
    if flat:
        for source in range(n * m):
            pl.when(place != source)(lambda: flat_from(source).wait())
    else:
        lax.fori_loop(1, m, finish(batch_copy), 0)
    total = jnp.sum(redb[...], axis=0)
    ga_out[...] = total[:, :heads]
    gbias_out[...] = turn(total, tokens - heads)[:, :heads]
    gskip_out[...] = turn(total, tokens - 2 * heads)[:, :heads]


def place_outputs(count, *refs):
    sems = refs[2 * count]
    copies = [
        pltpu.make_async_copy(refs[i], refs[count + i], sems.at[i]) for i in range(count)
    ]
    for copy in copies:
        copy.start()
    for copy in copies:
        copy.wait()


def shards(dt_raw, dt_bias, a_log, d_skip, x_in, b_in, c_in, cotangent):
    n, m = lax.axis_size("seq"), lax.axis_size("batch")
    _, tokens, heads = dt_raw.shape
    channels = x_in.shape[2]
    state = b_in.shape[2]
    chunks = channels // WIDTH
    steps = n * m if n * m <= FLAT else m - 1
    big = (chunks, tokens, WIDTH)
    square = (tokens, tokens)
    vmem = pl.BlockSpec(memory_space=pltpu.VMEM)
    hbm = pl.BlockSpec(memory_space=pltpu.HBM)
    dma = pltpu.SemaphoreType.DMA
    shape = jax.ShapeDtypeStruct
    made = pl.pallas_call(
        functools.partial(kernel, n, m, heads, tokens),
        out_shape=(
            shape((tokens, channels), BF16),
            shape((tokens, channels), BF16),
            shape((tokens, state), BF16),
            shape((tokens, state), BF16),
            shape((heads, tokens), F32),
        ) + (shape((1, heads), F32),) * 3,
        in_specs=[hbm] * 8,
        out_specs=(vmem,) * 8,
        scratch_shapes=[
            pltpu.VMEM((heads, tokens), F32),
            pltpu.VMEM((1, heads), F32),
            pltpu.VMEM((1, heads), F32),
            pltpu.VMEM((1, heads), F32),
            pltpu.VMEM((tokens, channels), BF16),
            pltpu.VMEM((tokens, state), BF16),
            pltpu.VMEM((tokens, state), BF16),
            pltpu.VMEM((tokens, channels), BF16),
            dma((8,)),
            pltpu.VMEM(square, F32),
            pltpu.VMEM((8, tokens), F32),
            pltpu.VMEM((2 * tokens + 16, tokens), BF16),
            pltpu.VMEM(square, BF16),
            pltpu.VMEM(square, F32),
            pltpu.VMEM((tokens, WIDTH), jnp.int32),
            pltpu.VMEM(square, F32),
            pltpu.VMEM((chunks, 8, WIDTH), F32),
            pltpu.VMEM(big, F32),
            pltpu.VMEM(big, F32),
            pltpu.VMEM(big, BF16),
            pltpu.VMEM(big, BF16),
            pltpu.VMEM(big, F32),
            pltpu.VMEM(big, F32),
            pltpu.VMEM(big, F32),
            pltpu.VMEM(big, F32),
            pltpu.VMEM(big, BF16),
            pltpu.VMEM(big, BF16),
            pltpu.VMEM(big, BF16),
            pltpu.VMEM(big, BF16),
            pltpu.VMEM(square, F32),
            pltpu.VMEM(square, F32),
            pltpu.VMEM(square, F32),
            pltpu.VMEM(square, F32),
            pltpu.VMEM(square, F32),
            pltpu.VMEM((8, tokens), F32),
            pltpu.VMEM(square, F32),
            pltpu.VMEM(square, F32),
            pltpu.VMEM(square, F32),
            pltpu.VMEM((n, 1, tokens), F32),
            pltpu.VMEM((n * m if n * m <= FLAT else m, 1, tokens), F32),
            dma((chunks,)), dma((chunks,)), dma((chunks,)), dma((chunks,)),
            dma((n - 1,)), dma((n - 1,)), dma((steps,)), dma((steps,)),
        ],
        compiler_params=pltpu.CompilerParams(
            collective_id=0, has_side_effects=True, vmem_limit_bytes=40 * 2**20),
    )(
        *(pltpu.with_memory_space_constraint(a, pltpu.HBM) for a in (
            dt_raw[0].T, dt_bias[None], a_log[None], d_skip[None],
            x_in[0], b_in[0], c_in[0], cotangent[0]))
    )
    out, gx, gb, gc, gdt, alog, bias, skip = pl.pallas_call(
        functools.partial(place_outputs, 8),
        out_shape=tuple(shape(a.shape, a.dtype) for a in made),
        in_specs=[vmem] * 8,
        out_specs=(hbm,) * 8,
        scratch_shapes=[dma((8,))],
        compiler_params=pltpu.CompilerParams(vmem_limit_bytes=4 * 2**20),
    )(*made)
    return (out[None], gx[None], gb[None], gc[None], gdt.T[None], alog[0], bias[0], skip[0])


def solution(mesh):
    rows = P("batch", "seq", None)
    return jax.shard_map(
        shards,
        mesh=mesh,
        in_specs=(rows, P(), P(), P(), rows, rows, rows, rows),
        out_specs=(rows, rows, rows, rows, rows, P(), P(), P()),
        check_vma=False,
    )
```

```python
import functools

import jax
import jax.numpy as jnp
from jax import lax
from jax.experimental import pallas as pl
from jax.experimental.pallas import tpu as pltpu
from jax.sharding import PartitionSpec as P

HEAD_DIM = 64
WIDTH = 256
F_LAG = 2
B_LAG = 3
UNROLL = 3
FLAT = 64
LOG2E = 1.4426950408889634
F32 = jnp.float32
BF16 = jnp.bfloat16


def mm(a, b):
    return jnp.dot(a, b, preferred_element_type=F32)


def mm_nt(a, b):
    return lax.dot_general(a, b, (((1,), (1,)), ((), ())), preferred_element_type=F32)


def exact(a, b):
    return jnp.dot(a, b, preferred_element_type=F32, precision=lax.Precision.HIGHEST)


def iota(shape, dim):
    return lax.broadcasted_iota(jnp.int32, shape, dim)


def split3(value, heads):
    high = value.astype(BF16).astype(F32)
    rest = value - high
    mid = rest.astype(BF16).astype(F32)
    low = (rest - mid).astype(BF16).astype(F32)
    packed = high + pltpu.roll(mid, heads, 1) + pltpu.roll(low, 2 * heads, 1)
    return packed.astype(BF16)


def kernel(
    n, m, heads, tokens,
    dt_hbm, bias_hbm, alog_hbm, skip_hbm, x_hbm, b_hbm, c_hbm, g_hbm,
    out_ref, gx_ref, gb_ref, gc_ref, gdt_ref, ga_out, gbias_out, gskip_out,
    dt_ref, bias_ref, alog_ref, skip_ref, x_ref, b_ref, c_ref, g_ref,
    in_sem, pad, prm, pk, apk, vt, kmod, cbm, ms, ee, we, wx, eg, sl, dc, vin, uin,
    fsend, car, bsend, ds,
    cum_ref, ratio, slow, rowa, cola, misc, dcb, gba, gca, reds, redb,
    fs_sem, fr_sem, bs_sem, br_sem, rs_send, rs_recv, rb_send, rb_recv,
):
    z = lax.axis_index("seq")
    w = lax.axis_index("batch")
    chunks = heads * HEAD_DIM // WIDTH
    per = WIDTH // HEAD_DIM

    fetches = [
        pltpu.make_async_copy(a, b, in_sem.at[i])
        for i, (a, b) in enumerate((
            (dt_hbm, dt_ref), (bias_hbm, bias_ref), (alog_hbm, alog_ref), (skip_hbm, skip_ref),
            (b_hbm, b_ref), (c_hbm, c_ref), (x_hbm, x_ref), (g_hbm, g_ref)))
    ]
    for fetch in fetches:
        fetch.start()
    barrier = pltpu.get_barrier_semaphore()

    def wrap(place, size):
        return jnp.where(place >= size, place - size, place)

    ring_z = [wrap(z + d, n) for d in range(n)]
    ring_w = [wrap(w + d, m) for d in range(m)]

    def other(d):
        return {"seq": ring_z[d // m], "batch": ring_w[d % m]}

    def greet_seq(d, _):
        pl.semaphore_signal(barrier, inc=1, device_id={"seq": lax.rem(z + d, n)},
                            device_id_type=pl.DeviceIdType.MESH)
        return 0

    def greet_batch(d, _):
        pl.semaphore_signal(barrier, inc=1, device_id={"batch": lax.rem(w + d, m)},
                            device_id_type=pl.DeviceIdType.MESH)
        return 0

    flat = n * m <= FLAT
    relay = flat and n > 3
    peers = n * m - 1 if flat else n + m - 2
    edge_peers = 1 if relay else peers
    if relay:
        @pl.when((z == 1) | (z == n - 2))
        def _():
            pl.semaphore_signal(
                barrier, inc=1, device_id={"seq": jnp.where(z == 1, 0, n - 1)},
                device_id_type=pl.DeviceIdType.MESH)

        for dw in range(m):
            for inner in range(1, n - 1):

                def greet():
                    pl.semaphore_signal(
                        barrier, inc=1, device_id={"seq": inner, "batch": ring_w[dw]},
                        device_id_type=pl.DeviceIdType.MESH)

                if dw:
                    greet()
                else:
                    pl.when(z != inner)(greet)
    elif flat:
        for d in range(1, n * m):
            pl.semaphore_signal(barrier, inc=1, device_id=other(d),
                                device_id_type=pl.DeviceIdType.MESH)
    else:
        lax.fori_loop(1, n, greet_seq, 0)
        lax.fori_loop(1, m, greet_batch, 0)

    def fcopy(i):
        return pltpu.make_async_remote_copy(
            src_ref=fsend.at[i], dst_ref=car.at[i], send_sem=fs_sem.at[i], recv_sem=fr_sem.at[i],
            device_id={"seq": jnp.minimum(z + 1, n - 1)}, device_id_type=pl.DeviceIdType.MESH)

    def bcopy(i):
        return pltpu.make_async_remote_copy(
            src_ref=bsend.at[i], dst_ref=ds.at[i], send_sem=bs_sem.at[i], recv_sem=br_sem.at[i],
            device_id={"seq": jnp.maximum(z - 1, 0)}, device_id_type=pl.DeviceIdType.MESH)

    pad[...] = jnp.zeros_like(pad)
    prm[...] = jnp.zeros_like(prm)
    for fetch in fetches[:6]:
        fetch.wait()
    pad[0:heads, :] = dt_ref[...]
    prm[0:1, :heads] = bias_ref[...]
    prm[1:2, :heads] = alog_ref[...]
    prm[2:3, :heads] = skip_ref[...]
    square = (tokens, tokens)
    is_head = iota(square, 1) < heads
    raw = pad[...].T + prm[0:1, :]
    step = jnp.maximum(raw, 0.0) + jnp.log1p(jnp.exp(-jnp.abs(raw)))
    rate = jnp.exp(prm[1:2, :])
    decay = jnp.where(is_head, -rate * step, 0.0)
    causal = iota(square, 0) >= iota(square, 1)
    slope = 1.0 / (1.0 + jnp.exp(-raw))
    cum = exact(jnp.where(causal, 1.0, 0.0), decay)
    last = cum[tokens - 1 : tokens, :]
    pk[0:tokens, :] = split3(jnp.where(is_head, jnp.exp(cum), 0.0), heads)
    pk[tokens : 2 * tokens, :] = split3(
        jnp.where(is_head, jnp.exp(last - cum) * step, 0.0), heads)
    head_row = is_head[0:1, :]
    factor = jnp.where(head_row, jnp.exp(last.astype(BF16).astype(F32)), 0.0)
    row16 = iota((16, tokens), 0)
    pk[2 * tokens : 2 * tokens + 16, :] = split3(
        jnp.where(row16 == 0, prm[2:3, :], 0.0) + jnp.where(row16 == 1, factor, 0.0), heads)
    k = iota((tokens, WIDTH), 0)
    kmod[...] = k - jnp.where(k >= heads, heads, 0) - jnp.where(k >= 2 * heads, heads, 0)
    b16 = b_ref[...]
    c16 = c_ref[...]
    bt = b16.astype(F32).T.astype(BF16)
    ct = c16.astype(F32).T.astype(BF16)

    for fetch in fetches[6:]:
        fetch.wait()
    edge = (z == 0) | (z == n - 1)
    place = z * m + w

    def cols(i):
        return pl.ds(pl.multiple_of(i * WIDTH, WIDTH), WIDTH)

    def state(i):
        group = lax.shift_right_logical(iota((tokens, WIDTH), 1), 6)
        spread = jnp.where(kmod[...] - group == i * per, 1.0, 0.0).astype(BF16)
        wide = mm(pk[...], spread)
        yield
        ee[i] = wide[0:tokens]
        we[i] = wide[tokens : 2 * tokens]
        ms[i] = wide[2 * tokens : 2 * tokens + 8]
        wx_i = (x_ref[:, cols(i)].astype(F32) * wide[tokens : 2 * tokens]).astype(BF16)
        eg_i = (g_ref[:, cols(i)].astype(F32) * wide[0:tokens]).astype(BF16)
        wx[i] = wx_i
        eg[i] = eg_i
        yield
        sl_i = mm(bt, wx_i)
        dc_i = mm(ct, eg_i)
        yield
        sl[i] = sl_i
        dc[i] = dc_i

    def together(*stages):
        stages = list(stages)
        while stages:
            stages = [stage for stage in stages if next(stage, 0) is None]

    def announce(i):
        @pl.when(z == 0)
        def _():
            car[i] = jnp.zeros((tokens, WIDTH), BF16)
            fsend[i] = sl[i].astype(BF16)
            fcopy(i).start()

        @pl.when(z == n - 1)
        def _():
            ds[i] = jnp.zeros((tokens, WIDTH), BF16)
            bsend[i] = dc[i].astype(BF16)
            bcopy(i).start()

    def states(k, _):
        together(*(state(1 + k * unroll + u) for u in range(unroll)))
        for u in range(unroll):
            announce(1 + k * unroll + u)
        return 0

    together(state(0))

    @pl.when(edge)
    def _():
        pl.semaphore_wait(barrier, edge_peers)

    announce(0)
    unroll = UNROLL if (chunks - 1) % UNROLL == 0 else 1
    lax.fori_loop(0, (chunks - 1) // unroll, states, 0)

    cum_ref[...] = cum
    ratio[...] = slope / step
    slow[...] = rate * exact(jnp.where(causal, 1.0, 0.0), slope)
    cum2 = cum * LOG2E
    apk[...] = split3(cum2, heads)
    vt[...] = (cum2 - jnp.log(step) * LOG2E).T
    cbm[...] = jnp.where(causal, mm(c16, bt), 0.0)
    for acc in (rowa, cola, misc, dcb, gba, gca):
        acc[...] = jnp.zeros_like(acc)

    @pl.when(jnp.logical_not(edge))
    def _():
        pl.semaphore_wait(barrier, peers)


    def to_heads(value, i):
        group = lax.shift_right_logical(iota((WIDTH, tokens), 0), 6)
        gather = jnp.where(iota((WIDTH, tokens), 1) - group == i * per, 1.0, 0.0).astype(BF16)
        high = value.astype(BF16)
        low = (value - high.astype(F32)).astype(BF16)
        return mm(high, gather) + mm(low, gather)

    def within(i):
        lane = iota(square, 1)
        left = jnp.where(lane < HEAD_DIM, 1.0, 0.0).astype(BF16)
        right = jnp.where(lane < HEAD_DIM, 0.0, 1.0).astype(BF16)
        second = jnp.where(iota((tokens, 2 * tokens), 1) < tokens, 0, 1)
        table = kmod[:, 0:1] - second
        count = WIDTH // 128
        heads_of = [i * per + 2 * q for q in range(count)]
        pairs = [pl.ds(pl.multiple_of(i * WIDTH + q * 128, 128), 128) for q in range(count)]
        xqs = [x_ref[:, pair] for pair in pairs]
        gqs = [g_ref[:, pair] for pair in pairs]
        xss = [jnp.concatenate([xq * left, xq * right], axis=0) for xq in xqs]
        gss = [jnp.concatenate([gq * left, gq * right], axis=0) for gq in gqs]
        logs = [
            mm(apk[...], jnp.where(table == head, 1.0, 0.0).astype(BF16)) for head in heads_of]
        gates = []
        for head, log in zip(heads_of, logs):
            v_row = jnp.concatenate([vt[pl.ds(head, 1), :], vt[pl.ds(head + 1, 1), :]], axis=1)
            gates.append(jnp.exp2(jnp.minimum(log - v_row, 100.0)))
        cb = cbm[...]
        scores = [
            [(gate[:, h * tokens : (h + 1) * tokens] * cb).astype(BF16) for h in range(2)]
            for gate in gates]
        turned = [jnp.concatenate([part.T for part in both], axis=1) for both in scores]
        grads = [mm_nt(gq, xs) * gate for gq, xs, gate in zip(gqs, xss, gates)]
        for q in range(count):
            vin[i, :, q * 128 : (q + 1) * 128] = mm(jnp.concatenate(scores[q], axis=1), xss[q])
            uin[i, :, q * 128 : (q + 1) * 128] = mm(turned[q], gss[q])
        total = grads[0][:, :tokens] + grads[0][:, tokens:]
        for grad in grads[1:]:
            total = total + grad[:, :tokens] + grad[:, tokens:]
        dcb[...] += total

    def forward(i):
        state_in = car[i]
        inter = mm(c16, state_in)
        to_c = mm_nt(eg[i], state_in)
        yield
        x_i = x_ref[:, cols(i)].astype(F32)
        v = vin[i] + ee[i] * inter
        out_ref[:, cols(i)] = (v + ms[i, 0:1, :] * x_i).astype(BF16)
        share = g_ref[:, cols(i)].astype(F32) * v
        yield
        share = to_heads(share, i)
        yield
        rowa[...] += share
        gca[...] += to_c

    def backward(i):
        state_in = ds[i]
        from_state = mm(b16, state_in)
        to_b = mm_nt(wx[i], state_in)
        yield
        g_i = g_ref[:, cols(i)].astype(F32)
        u = uin[i]
        gx_ref[:, cols(i)] = (u + we[i] * from_state + ms[i, 0:1, :] * g_i).astype(BF16)
        share = x_ref[:, cols(i)].astype(F32) * u + wx[i].astype(F32) * from_state
        yield
        share = to_heads(share, i)
        yield
        cola[...] += share
        gba[...] += to_b

    def sums(i):
        onward = ms[i, 1:2, :] * car[i].astype(F32) + sl[i]
        d_last = jnp.sum(onward * ds[i].astype(F32), axis=0, keepdims=True)
        d_skip = jnp.sum(
            g_ref[:, cols(i)].astype(F32) * x_ref[:, cols(i)].astype(F32), axis=0, keepdims=True)
        row = iota((8, WIDTH), 0)
        both = jnp.where(row == 0, d_last, 0.0) + jnp.where(row == 1, d_skip, 0.0)
        yield
        both = to_heads(both, i)
        yield
        misc[...] += both

    cases = set()
    for row in range(n):
        for j in range(chunks + max(F_LAG, B_LAG) * max(n - 2, 0)):
            f = j - F_LAG * max(row - 1, 0)
            b = j - B_LAG * max(n - 2 - row, 0)
            marks = (0 <= f < chunks, 0 <= b < chunks, 0 <= min(f, b) < chunks)
            cases.add(sum(1 << k for k, mark in enumerate(marks) if mark))
    cases = sorted(cases - {0})

    def advance(j, _):
        f = j - F_LAG * jnp.maximum(z - 1, 0)
        b = j - B_LAG * jnp.maximum(n - 2 - z, 0)
        both = jnp.minimum(f, b)
        f_on = (f >= 0) & (f < chunks)
        b_on = (b >= 0) & (b < chunks)

        @pl.when(f_on & (z > 0))
        def _():
            fcopy(f).wait_recv()
            fsend[f] = (ms[f, 1:2, :] * car[f].astype(F32) + sl[f]).astype(BF16)

        @pl.when(f_on & (z > 0) & (z < n - 1))
        def _():
            fcopy(f).start()

        @pl.when(j < chunks)
        def _():
            within(j)

        @pl.when(b_on & (z < n - 1))
        def _():
            bcopy(b).wait_recv()

        @pl.when(b_on & (z < n - 1) & (z > 0))
        def _():
            bsend[b] = (ms[b, 1:2, :] * ds[b].astype(F32) + dc[b]).astype(BF16)
            bcopy(b).start()

        kind = (
            jnp.where(f_on, 1, 0) + jnp.where(b_on, 2, 0)
            + jnp.where((both >= 0) & (both < chunks), 4, 0)
        )
        for case in cases:

            @pl.when(kind == case)
            def _():
                together(*(
                    part(i) for bit, part, i in ((1, forward, f), (2, backward, b), (4, sums, both))
                    if case & bit))

        return 0

    lax.fori_loop(0, chunks + max(F_LAG, B_LAG) * max(n - 2, 0), advance, 0)

    d_cum = rowa[...] - cola[...]
    d_cum = d_cum + jnp.where(iota(square, 0) == tokens - 1, misc[0:1, :], 0.0)
    grad_a = jnp.sum(d_cum * cum_ref[...], axis=0, keepdims=True)
    grad_bias = jnp.sum(cola[...] * ratio[...] - d_cum * slow[...], axis=0, keepdims=True)

    def turn(row, by):
        return pltpu.roll(jnp.broadcast_to(row, (8, tokens)), by, 1)[0:1, :]

    def per_head(row):
        return jnp.where(head_row, row, 0.0)

    mine = (
        per_head(grad_a) + turn(per_head(grad_bias), heads)
        + turn(per_head(misc[1:2, :]), 2 * heads)
    )

    def seq_copy(d):
        return pltpu.make_async_remote_copy(
            src_ref=reds.at[z], dst_ref=reds.at[z], send_sem=rs_send.at[d - 1],
            recv_sem=rs_recv.at[d - 1], device_id={"seq": lax.rem(z + d, n)},
            device_id_type=pl.DeviceIdType.MESH)

    def batch_copy(d):
        return pltpu.make_async_remote_copy(
            src_ref=redb.at[w], dst_ref=redb.at[w], send_sem=rb_send.at[d - 1],
            recv_sem=rb_recv.at[d - 1], device_id={"batch": lax.rem(w + d, m)},
            device_id_type=pl.DeviceIdType.MESH)

    def flat_copy(to):
        return pltpu.make_async_remote_copy(
            src_ref=redb.at[place], dst_ref=redb.at[place], send_sem=rb_send.at[to],
            recv_sem=rb_recv.at[place],
            device_id={"seq": jnp.int32(to // m), "batch": jnp.int32(to % m)},
            device_id_type=pl.DeviceIdType.MESH)

    def flat_from(source):
        return pltpu.make_async_remote_copy(
            src_ref=redb.at[source], dst_ref=redb.at[source], send_sem=rb_send.at[source],
            recv_sem=rb_recv.at[source],
            device_id={"seq": jnp.int32(source // m), "batch": jnp.int32(source % m)},
            device_id_type=pl.DeviceIdType.MESH)

    def start(copy):
        return lambda d, _: (copy(d).start(), 0)[1]

    def finish(copy):
        return lambda d, _: (copy(d).wait(), 0)[1]

    if flat:
        redb[place] = mine
        for to in range(n * m):
            pl.when(place != to)(lambda: flat_copy(to).start())
    else:
        reds[z] = mine
        lax.fori_loop(1, n, start(seq_copy), 0)
    later = iota(square, 0) <= iota(square, 1)
    d_decay = exact(jnp.where(later, 1.0, 0.0), d_cum)
    d_raw = cola[...] * ratio[...] - rate * slope * d_decay
    gdt_ref[...] = d_raw.T[0:heads, :]
    d_cb = jnp.where(causal, dcb[...], 0.0)
    gc_ref[...] = (gca[...] + mm(d_cb.astype(BF16), b16)).astype(BF16)
    gb_ref[...] = (gba[...] + mm(d_cb.T.astype(BF16), c16)).astype(BF16)
    if not flat:
        lax.fori_loop(1, n, finish(seq_copy), 0)
        redb[w] = lax.fori_loop(0, n, lambda i, t: t + reds[i], jnp.zeros((1, tokens), F32))
        lax.fori_loop(1, m, start(batch_copy), 0)

    def drain(i, _):
        @pl.when(z < n - 1)
        def _():
            fcopy(i).wait_send()

        @pl.when(z > 0)
        def _():
            bcopy(i).wait_send()

        return 0

    lax.fori_loop(0, chunks, drain, 0)
    if flat:
        for source in range(n * m):
            pl.when(place != source)(lambda: flat_from(source).wait())
    else:
        lax.fori_loop(1, m, finish(batch_copy), 0)
    total = jnp.sum(redb[...], axis=0)
    ga_out[...] = total[:, :heads]
    gbias_out[...] = turn(total, tokens - heads)[:, :heads]
    gskip_out[...] = turn(total, tokens - 2 * heads)[:, :heads]


def place_outputs(count, *refs):
    sems = refs[2 * count]
    copies = [
        pltpu.make_async_copy(refs[i], refs[count + i], sems.at[i]) for i in range(count)
    ]
    for copy in copies:
        copy.start()
    for copy in copies:
        copy.wait()


def shards(dt_raw, dt_bias, a_log, d_skip, x_in, b_in, c_in, cotangent):
    n, m = lax.axis_size("seq"), lax.axis_size("batch")
    _, tokens, heads = dt_raw.shape
    channels = x_in.shape[2]
    state = b_in.shape[2]
    chunks = channels // WIDTH
    steps = n * m if n * m <= FLAT else m - 1
    big = (chunks, tokens, WIDTH)
    square = (tokens, tokens)
    vmem = pl.BlockSpec(memory_space=pltpu.VMEM)
    hbm = pl.BlockSpec(memory_space=pltpu.HBM)
    dma = pltpu.SemaphoreType.DMA
    shape = jax.ShapeDtypeStruct
    made = pl.pallas_call(
        functools.partial(kernel, n, m, heads, tokens),
        out_shape=(
            shape((tokens, channels), BF16),
            shape((tokens, channels), BF16),
            shape((tokens, state), BF16),
            shape((tokens, state), BF16),
            shape((heads, tokens), F32),
        ) + (shape((1, heads), F32),) * 3,
        in_specs=[hbm] * 8,
        out_specs=(vmem,) * 8,
        scratch_shapes=[
            pltpu.VMEM((heads, tokens), F32),
            pltpu.VMEM((1, heads), F32),
            pltpu.VMEM((1, heads), F32),
            pltpu.VMEM((1, heads), F32),
            pltpu.VMEM((tokens, channels), BF16),
            pltpu.VMEM((tokens, state), BF16),
            pltpu.VMEM((tokens, state), BF16),
            pltpu.VMEM((tokens, channels), BF16),
            dma((8,)),
            pltpu.VMEM(square, F32),
            pltpu.VMEM((8, tokens), F32),
            pltpu.VMEM((2 * tokens + 16, tokens), BF16),
            pltpu.VMEM(square, BF16),
            pltpu.VMEM(square, F32),
            pltpu.VMEM((tokens, WIDTH), jnp.int32),
            pltpu.VMEM(square, F32),
            pltpu.VMEM((chunks, 8, WIDTH), F32),
            pltpu.VMEM(big, F32),
            pltpu.VMEM(big, F32),
            pltpu.VMEM(big, BF16),
            pltpu.VMEM(big, BF16),
            pltpu.VMEM(big, F32),
            pltpu.VMEM(big, F32),
            pltpu.VMEM(big, F32),
            pltpu.VMEM(big, F32),
            pltpu.VMEM(big, BF16),
            pltpu.VMEM(big, BF16),
            pltpu.VMEM(big, BF16),
            pltpu.VMEM(big, BF16),
            pltpu.VMEM(square, F32),
            pltpu.VMEM(square, F32),
            pltpu.VMEM(square, F32),
            pltpu.VMEM(square, F32),
            pltpu.VMEM(square, F32),
            pltpu.VMEM((8, tokens), F32),
            pltpu.VMEM(square, F32),
            pltpu.VMEM(square, F32),
            pltpu.VMEM(square, F32),
            pltpu.VMEM((n, 1, tokens), F32),
            pltpu.VMEM((n * m if n * m <= FLAT else m, 1, tokens), F32),
            dma((chunks,)), dma((chunks,)), dma((chunks,)), dma((chunks,)),
            dma((n - 1,)), dma((n - 1,)), dma((steps,)), dma((steps,)),
        ],
        compiler_params=pltpu.CompilerParams(
            collective_id=0, has_side_effects=True, vmem_limit_bytes=40 * 2**20),
    )(
        *(pltpu.with_memory_space_constraint(a, pltpu.HBM) for a in (
            dt_raw[0].T, dt_bias[None], a_log[None], d_skip[None],
            x_in[0], b_in[0], c_in[0], cotangent[0]))
    )
    out, gx, gb, gc, gdt, alog, bias, skip = pl.pallas_call(
        functools.partial(place_outputs, 8),
        out_shape=tuple(shape(a.shape, a.dtype) for a in made),
        in_specs=[vmem] * 8,
        out_specs=(hbm,) * 8,
        scratch_shapes=[dma((8,))],
        compiler_params=pltpu.CompilerParams(vmem_limit_bytes=4 * 2**20),
    )(*made)
    return (out[None], gx[None], gb[None], gc[None], gdt.T[None], alog[0], bias[0], skip[0])


def solution(mesh):
    rows = P("batch", "seq", None)
    return jax.shard_map(
        shards,
        mesh=mesh,
        in_specs=(rows, P(), P(), P(), rows, rows, rows, rows),
        out_specs=(rows, rows, rows, rows, rows, P(), P(), P()),
        check_vma=False,
    )
```

```python
import functools

import jax
import jax.numpy as jnp
from jax import lax
from jax.experimental import pallas as pl
from jax.experimental.pallas import tpu as pltpu
from jax.sharding import PartitionSpec as P

HEAD_DIM = 64
WIDTH = 256
F_LAG = 2
B_LAG = 3
UNROLL = 3
FLAT = 64
LOG2E = 1.4426950408889634
F32 = jnp.float32
BF16 = jnp.bfloat16


def mm(a, b):
    return jnp.dot(a, b, preferred_element_type=F32)


def mm_nt(a, b):
    return lax.dot_general(a, b, (((1,), (1,)), ((), ())), preferred_element_type=F32)


def exact(a, b):
    return jnp.dot(a, b, preferred_element_type=F32, precision=lax.Precision.HIGHEST)


def iota(shape, dim):
    return lax.broadcasted_iota(jnp.int32, shape, dim)


def split3(value, heads):
    high = value.astype(BF16).astype(F32)
    rest = value - high
    mid = rest.astype(BF16).astype(F32)
    low = (rest - mid).astype(BF16).astype(F32)
    packed = high + pltpu.roll(mid, heads, 1) + pltpu.roll(low, 2 * heads, 1)
    return packed.astype(BF16)


def kernel(
    n, m, heads, tokens,
    dt_hbm, bias_hbm, alog_hbm, skip_hbm, x_hbm, b_hbm, c_hbm, g_hbm,
    out_ref, gx_ref, gb_ref, gc_ref, gdt_ref, ga_out, gbias_out, gskip_out,
    dt_ref, bias_ref, alog_ref, skip_ref, x_ref, b_ref, c_ref, g_ref,
    in_sem, x_sem, g_sem, pad, prm, pk, apk, vt, kmod, cbm, ms, ee, we, wx, eg, sl, dc, vin, uin,
    fsend, car, bsend, ds,
    cum_ref, ratio, slow, rowa, cola, misc, dcb, gba, gca, reds, redb,
    fs_sem, fr_sem, bs_sem, br_sem, rs_send, rs_recv, rb_send, rb_recv,
):
    z = lax.axis_index("seq")
    w = lax.axis_index("batch")
    chunks = heads * HEAD_DIM // WIDTH
    per = WIDTH // HEAD_DIM

    unroll = UNROLL if (chunks - 1) % UNROLL == 0 else 1
    groups = 1 + (chunks - 1) // unroll
    small = [
        pltpu.make_async_copy(a, b, in_sem.at[i])
        for i, (a, b) in enumerate((
            (dt_hbm, dt_ref), (bias_hbm, bias_ref), (alog_hbm, alog_ref), (skip_hbm, skip_ref),
            (b_hbm, b_ref), (c_hbm, c_ref)))
    ]

    def fetch(k, first):
        size = WIDTH if first else unroll * WIDTH
        low = 0 if first else pl.multiple_of(WIDTH + (k - 1) * unroll * WIDTH, WIDTH)
        part = pl.ds(low, size)
        return (
            pltpu.make_async_copy(x_hbm.at[:, part], x_ref.at[:, part], x_sem.at[k]),
            pltpu.make_async_copy(g_hbm.at[:, part], g_ref.at[:, part], g_sem.at[k]),
        )

    def fetch_small():
        for copy in small:
            copy.start()
        for copy in fetch(0, True):
            copy.start()

    barrier = pltpu.get_barrier_semaphore()

    def wrap(place, size):
        return jnp.where(place >= size, place - size, place)

    ring_z = [wrap(z + d, n) for d in range(n)]
    ring_w = [wrap(w + d, m) for d in range(m)]

    def other(d):
        return {"seq": ring_z[d // m], "batch": ring_w[d % m]}

    def greet_seq(d, _):
        pl.semaphore_signal(barrier, inc=1, device_id={"seq": lax.rem(z + d, n)},
                            device_id_type=pl.DeviceIdType.MESH)
        return 0

    def greet_batch(d, _):
        pl.semaphore_signal(barrier, inc=1, device_id={"batch": lax.rem(w + d, m)},
                            device_id_type=pl.DeviceIdType.MESH)
        return 0

    flat = n * m <= FLAT
    relay = flat and n > 3
    peers = n * m - 1 if flat else n + m - 2
    edge_peers = 1 if relay else peers
    if not relay:
        fetch_small()
    if relay:
        @pl.when((z == 1) | (z == n - 2))
        def _():
            pl.semaphore_signal(
                barrier, inc=1, device_id={"seq": jnp.where(z == 1, 0, n - 1)},
                device_id_type=pl.DeviceIdType.MESH)

        fetch_small()
        for dw in range(m):
            for inner in range(1, n - 1):

                def greet():
                    pl.semaphore_signal(
                        barrier, inc=1, device_id={"seq": inner, "batch": ring_w[dw]},
                        device_id_type=pl.DeviceIdType.MESH)

                if dw:
                    greet()
                else:
                    pl.when(z != inner)(greet)
    elif flat:
        for d in range(1, n * m):
            pl.semaphore_signal(barrier, inc=1, device_id=other(d),
                                device_id_type=pl.DeviceIdType.MESH)
    else:
        lax.fori_loop(1, n, greet_seq, 0)
        lax.fori_loop(1, m, greet_batch, 0)

    for k in range(1, groups):
        for copy in fetch(k, False):
            copy.start()

    def fcopy(i):
        return pltpu.make_async_remote_copy(
            src_ref=fsend.at[i], dst_ref=car.at[i], send_sem=fs_sem.at[0], recv_sem=fr_sem.at[i],
            device_id={"seq": jnp.minimum(z + 1, n - 1)}, device_id_type=pl.DeviceIdType.MESH)

    def bcopy(i):
        return pltpu.make_async_remote_copy(
            src_ref=bsend.at[i], dst_ref=ds.at[i], send_sem=bs_sem.at[0], recv_sem=br_sem.at[i],
            device_id={"seq": jnp.maximum(z - 1, 0)}, device_id_type=pl.DeviceIdType.MESH)

    pad[...] = jnp.zeros_like(pad)
    prm[...] = jnp.zeros_like(prm)
    for copy in small:
        copy.wait()
    pad[0:heads, :] = dt_ref[...]
    prm[0:1, :heads] = bias_ref[...]
    prm[1:2, :heads] = alog_ref[...]
    prm[2:3, :heads] = skip_ref[...]
    square = (tokens, tokens)
    is_head = iota(square, 1) < heads
    raw = pad[...].T + prm[0:1, :]
    step = jnp.maximum(raw, 0.0) + jnp.log1p(jnp.exp(-jnp.abs(raw)))
    rate = jnp.exp(prm[1:2, :])
    decay = jnp.where(is_head, -rate * step, 0.0)
    causal = iota(square, 0) >= iota(square, 1)
    slope = 1.0 / (1.0 + jnp.exp(-raw))
    cum = exact(jnp.where(causal, 1.0, 0.0), decay)
    last = cum[tokens - 1 : tokens, :]
    pk[0:tokens, :] = split3(jnp.where(is_head, jnp.exp(cum), 0.0), heads)
    pk[tokens : 2 * tokens, :] = split3(
        jnp.where(is_head, jnp.exp(last - cum) * step, 0.0), heads)
    head_row = is_head[0:1, :]
    factor = jnp.where(head_row, jnp.exp(last.astype(BF16).astype(F32)), 0.0)
    row16 = iota((16, tokens), 0)
    pk[2 * tokens : 2 * tokens + 16, :] = split3(
        jnp.where(row16 == 0, prm[2:3, :], 0.0) + jnp.where(row16 == 1, factor, 0.0), heads)
    k = iota((tokens, WIDTH), 0)
    kmod[...] = k - jnp.where(k >= heads, heads, 0) - jnp.where(k >= 2 * heads, heads, 0)
    b16 = b_ref[...]
    c16 = c_ref[...]
    bt = b16.astype(F32).T.astype(BF16)
    ct = c16.astype(F32).T.astype(BF16)

    edge = (z == 0) | (z == n - 1)
    place = z * m + w

    def cols(i):
        return pl.ds(pl.multiple_of(i * WIDTH, WIDTH), WIDTH)

    def state(i):
        group = lax.shift_right_logical(iota((tokens, WIDTH), 1), 6)
        spread = jnp.where(kmod[...] - group == i * per, 1.0, 0.0).astype(BF16)
        wide = mm(pk[...], spread)
        yield
        ee[i] = wide[0:tokens]
        we[i] = wide[tokens : 2 * tokens]
        ms[i] = wide[2 * tokens : 2 * tokens + 8]
        wx_i = (x_ref[:, cols(i)].astype(F32) * wide[tokens : 2 * tokens]).astype(BF16)
        eg_i = (g_ref[:, cols(i)].astype(F32) * wide[0:tokens]).astype(BF16)
        wx[i] = wx_i
        eg[i] = eg_i
        yield
        sl_i = mm(bt, wx_i)
        dc_i = mm(ct, eg_i)
        yield
        sl[i] = sl_i
        dc[i] = dc_i

    def together(*stages):
        stages = list(stages)
        while stages:
            stages = [stage for stage in stages if next(stage, 0) is None]

    def announce(i):
        @pl.when(z == 0)
        def _():
            car[i] = jnp.zeros((tokens, WIDTH), BF16)
            fsend[i] = sl[i].astype(BF16)
            fcopy(i).start()

        @pl.when(z == n - 1)
        def _():
            ds[i] = jnp.zeros((tokens, WIDTH), BF16)
            bsend[i] = dc[i].astype(BF16)
            bcopy(i).start()

    def states(k, _):
        for copy in fetch(1 + k, False):
            copy.wait()
        together(*(state(1 + k * unroll + u) for u in range(unroll)))
        for u in range(unroll):
            announce(1 + k * unroll + u)
        return 0

    for copy in fetch(0, True):
        copy.wait()
    together(state(0))

    @pl.when(edge)
    def _():
        pl.semaphore_wait(barrier, edge_peers)

    announce(0)
    lax.fori_loop(0, (chunks - 1) // unroll, states, 0)

    cum_ref[...] = cum
    ratio[...] = slope / step
    slow[...] = rate * exact(jnp.where(causal, 1.0, 0.0), slope)
    cum2 = cum * LOG2E
    apk[...] = split3(cum2, heads)
    vt[...] = (cum2 - jnp.log(step) * LOG2E).T
    cbm[...] = jnp.where(causal, mm(c16, bt), 0.0)
    for acc in (rowa, cola, misc, dcb, gba, gca):
        acc[...] = jnp.zeros_like(acc)

    @pl.when(jnp.logical_not(edge))
    def _():
        pl.semaphore_wait(barrier, peers)


    def to_heads(value, i):
        group = lax.shift_right_logical(iota((WIDTH, tokens), 0), 6)
        gather = jnp.where(iota((WIDTH, tokens), 1) - group == i * per, 1.0, 0.0).astype(BF16)
        high = value.astype(BF16)
        low = (value - high.astype(F32)).astype(BF16)
        return mm(high, gather) + mm(low, gather)

    def within(i):
        lane = iota(square, 1)
        left = jnp.where(lane < HEAD_DIM, 1.0, 0.0).astype(BF16)
        right = jnp.where(lane < HEAD_DIM, 0.0, 1.0).astype(BF16)
        second = jnp.where(iota((tokens, 2 * tokens), 1) < tokens, 0, 1)
        table = kmod[:, 0:1] - second
        count = WIDTH // 128
        heads_of = [i * per + 2 * q for q in range(count)]
        pairs = [pl.ds(pl.multiple_of(i * WIDTH + q * 128, 128), 128) for q in range(count)]
        xqs = [x_ref[:, pair] for pair in pairs]
        gqs = [g_ref[:, pair] for pair in pairs]
        xss = [jnp.concatenate([xq * left, xq * right], axis=0) for xq in xqs]
        gss = [jnp.concatenate([gq * left, gq * right], axis=0) for gq in gqs]
        logs = [
            mm(apk[...], jnp.where(table == head, 1.0, 0.0).astype(BF16)) for head in heads_of]
        gates = []
        for head, log in zip(heads_of, logs):
            v_row = jnp.concatenate([vt[pl.ds(head, 1), :], vt[pl.ds(head + 1, 1), :]], axis=1)
            gates.append(jnp.exp2(jnp.minimum(log - v_row, 100.0)))
        cb = cbm[...]
        scores = [
            [(gate[:, h * tokens : (h + 1) * tokens] * cb).astype(BF16) for h in range(2)]
            for gate in gates]
        turned = [jnp.concatenate([part.T for part in both], axis=1) for both in scores]
        grads = [mm_nt(gq, xs) * gate for gq, xs, gate in zip(gqs, xss, gates)]
        for q in range(count):
            vin[i, :, q * 128 : (q + 1) * 128] = mm(jnp.concatenate(scores[q], axis=1), xss[q])
            uin[i, :, q * 128 : (q + 1) * 128] = mm(turned[q], gss[q])
        total = grads[0][:, :tokens] + grads[0][:, tokens:]
        for grad in grads[1:]:
            total = total + grad[:, :tokens] + grad[:, tokens:]
        dcb[...] += total

    def forward(i):
        state_in = car[i]
        inter = mm(c16, state_in)
        to_c = mm_nt(eg[i], state_in)
        yield
        x_i = x_ref[:, cols(i)].astype(F32)
        v = vin[i] + ee[i] * inter
        out_ref[:, cols(i)] = (v + ms[i, 0:1, :] * x_i).astype(BF16)
        share = g_ref[:, cols(i)].astype(F32) * v
        yield
        share = to_heads(share, i)
        yield
        rowa[...] += share
        gca[...] += to_c

    def backward(i):
        state_in = ds[i]
        from_state = mm(b16, state_in)
        to_b = mm_nt(wx[i], state_in)
        yield
        g_i = g_ref[:, cols(i)].astype(F32)
        u = uin[i]
        gx_ref[:, cols(i)] = (u + we[i] * from_state + ms[i, 0:1, :] * g_i).astype(BF16)
        share = x_ref[:, cols(i)].astype(F32) * u + wx[i].astype(F32) * from_state
        yield
        share = to_heads(share, i)
        yield
        cola[...] += share
        gba[...] += to_b

    def sums(i):
        onward = ms[i, 1:2, :] * car[i].astype(F32) + sl[i]
        d_last = jnp.sum(onward * ds[i].astype(F32), axis=0, keepdims=True)
        d_skip = jnp.sum(
            g_ref[:, cols(i)].astype(F32) * x_ref[:, cols(i)].astype(F32), axis=0, keepdims=True)
        row = iota((8, WIDTH), 0)
        both = jnp.where(row == 0, d_last, 0.0) + jnp.where(row == 1, d_skip, 0.0)
        yield
        both = to_heads(both, i)
        yield
        misc[...] += both

    cases = set()
    for row in range(n):
        for j in range(chunks + max(F_LAG, B_LAG) * max(n - 2, 0)):
            f = j - F_LAG * max(row - 1, 0)
            b = j - B_LAG * max(n - 2 - row, 0)
            marks = (0 <= f < chunks, 0 <= b < chunks, 0 <= min(f, b) < chunks)
            cases.add(sum(1 << k for k, mark in enumerate(marks) if mark))
    cases = sorted(cases - {0})

    def advance(j, _):
        f = j - F_LAG * jnp.maximum(z - 1, 0)
        b = j - B_LAG * jnp.maximum(n - 2 - z, 0)
        both = jnp.minimum(f, b)
        f_on = (f >= 0) & (f < chunks)
        b_on = (b >= 0) & (b < chunks)

        @pl.when(f_on & (z > 0))
        def _():
            fcopy(f).wait_recv()
            fsend[f] = (ms[f, 1:2, :] * car[f].astype(F32) + sl[f]).astype(BF16)

        @pl.when(f_on & (z > 0) & (z < n - 1))
        def _():
            fcopy(f).start()

        @pl.when(j < chunks)
        def _():
            within(j)

        @pl.when(b_on & (z < n - 1))
        def _():
            bcopy(b).wait_recv()

        @pl.when(b_on & (z < n - 1) & (z > 0))
        def _():
            bsend[b] = (ms[b, 1:2, :] * ds[b].astype(F32) + dc[b]).astype(BF16)
            bcopy(b).start()

        kind = (
            jnp.where(f_on, 1, 0) + jnp.where(b_on, 2, 0)
            + jnp.where((both >= 0) & (both < chunks), 4, 0)
        )
        for case in cases:

            @pl.when(kind == case)
            def _():
                together(*(
                    part(i) for bit, part, i in ((1, forward, f), (2, backward, b), (4, sums, both))
                    if case & bit))

        return 0

    lax.fori_loop(0, chunks + max(F_LAG, B_LAG) * max(n - 2, 0), advance, 0)

    d_cum = rowa[...] - cola[...]
    d_cum = d_cum + jnp.where(iota(square, 0) == tokens - 1, misc[0:1, :], 0.0)
    grad_a = jnp.sum(d_cum * cum_ref[...], axis=0, keepdims=True)
    grad_bias = jnp.sum(cola[...] * ratio[...] - d_cum * slow[...], axis=0, keepdims=True)

    def turn(row, by):
        return pltpu.roll(jnp.broadcast_to(row, (8, tokens)), by, 1)[0:1, :]

    def per_head(row):
        return jnp.where(head_row, row, 0.0)

    mine = (
        per_head(grad_a) + turn(per_head(grad_bias), heads)
        + turn(per_head(misc[1:2, :]), 2 * heads)
    )

    def seq_copy(d):
        return pltpu.make_async_remote_copy(
            src_ref=reds.at[z], dst_ref=reds.at[z], send_sem=rs_send.at[d - 1],
            recv_sem=rs_recv.at[d - 1], device_id={"seq": lax.rem(z + d, n)},
            device_id_type=pl.DeviceIdType.MESH)

    def batch_copy(d):
        return pltpu.make_async_remote_copy(
            src_ref=redb.at[w], dst_ref=redb.at[w], send_sem=rb_send.at[d - 1],
            recv_sem=rb_recv.at[d - 1], device_id={"batch": lax.rem(w + d, m)},
            device_id_type=pl.DeviceIdType.MESH)

    def flat_copy(to):
        return pltpu.make_async_remote_copy(
            src_ref=redb.at[place], dst_ref=redb.at[place], send_sem=rb_send.at[0],
            recv_sem=rb_recv.at[0],
            device_id={"seq": jnp.int32(to // m), "batch": jnp.int32(to % m)},
            device_id_type=pl.DeviceIdType.MESH)

    def flat_wait(sem):
        rows = redb.at[pl.ds(0, n * m - 1)]
        pltpu.make_async_copy(rows, rows, sem).wait()

    def start(copy):
        return lambda d, _: (copy(d).start(), 0)[1]

    def finish(copy):
        return lambda d, _: (copy(d).wait(), 0)[1]

    if flat:
        redb[place] = mine
        for to in range(n * m):
            pl.when(place != to)(lambda: flat_copy(to).start())
    else:
        reds[z] = mine
        lax.fori_loop(1, n, start(seq_copy), 0)
    later = iota(square, 0) <= iota(square, 1)
    d_decay = exact(jnp.where(later, 1.0, 0.0), d_cum)
    d_raw = cola[...] * ratio[...] - rate * slope * d_decay
    gdt_ref[...] = d_raw.T[0:heads, :]
    d_cb = jnp.where(causal, dcb[...], 0.0)
    gc_ref[...] = (gca[...] + mm(d_cb.astype(BF16), b16)).astype(BF16)
    gb_ref[...] = (gba[...] + mm(d_cb.T.astype(BF16), c16)).astype(BF16)
    if not flat:
        lax.fori_loop(1, n, finish(seq_copy), 0)
        redb[w] = lax.fori_loop(0, n, lambda i, t: t + reds[i], jnp.zeros((1, tokens), F32))
        lax.fori_loop(1, m, start(batch_copy), 0)

    @pl.when(z < n - 1)
    def _():
        pltpu.make_async_copy(fsend, fsend, fs_sem.at[0]).wait()

    @pl.when(z > 0)
    def _():
        pltpu.make_async_copy(bsend, bsend, bs_sem.at[0]).wait()

    if flat:
        flat_wait(rb_send.at[0])
        flat_wait(rb_recv.at[0])
    else:
        lax.fori_loop(1, m, finish(batch_copy), 0)
    total = jnp.sum(redb[...], axis=0)
    ga_out[...] = total[:, :heads]
    gbias_out[...] = turn(total, tokens - heads)[:, :heads]
    gskip_out[...] = turn(total, tokens - 2 * heads)[:, :heads]


def place_outputs(count, *refs):
    sems = refs[2 * count]
    copies = [
        pltpu.make_async_copy(refs[i], refs[count + i], sems.at[i]) for i in range(count)
    ]
    for copy in copies:
        copy.start()
    for copy in copies:
        copy.wait()


def shards(dt_raw, dt_bias, a_log, d_skip, x_in, b_in, c_in, cotangent):
    n, m = lax.axis_size("seq"), lax.axis_size("batch")
    _, tokens, heads = dt_raw.shape
    channels = x_in.shape[2]
    state = b_in.shape[2]
    chunks = channels // WIDTH
    steps = 1 if n * m <= FLAT else m - 1
    stops = 1 if n * m <= FLAT else n - 1
    groups = 1 + (chunks - 1) // (UNROLL if (chunks - 1) % UNROLL == 0 else 1)
    big = (chunks, tokens, WIDTH)
    square = (tokens, tokens)
    vmem = pl.BlockSpec(memory_space=pltpu.VMEM)
    hbm = pl.BlockSpec(memory_space=pltpu.HBM)
    dma = pltpu.SemaphoreType.DMA
    shape = jax.ShapeDtypeStruct
    made = pl.pallas_call(
        functools.partial(kernel, n, m, heads, tokens),
        out_shape=(
            shape((tokens, channels), BF16),
            shape((tokens, channels), BF16),
            shape((tokens, state), BF16),
            shape((tokens, state), BF16),
            shape((heads, tokens), F32),
        ) + (shape((1, heads), F32),) * 3,
        in_specs=[hbm] * 8,
        out_specs=(vmem,) * 8,
        scratch_shapes=[
            pltpu.VMEM((heads, tokens), F32),
            pltpu.VMEM((1, heads), F32),
            pltpu.VMEM((1, heads), F32),
            pltpu.VMEM((1, heads), F32),
            pltpu.VMEM((tokens, channels), BF16),
            pltpu.VMEM((tokens, state), BF16),
            pltpu.VMEM((tokens, state), BF16),
            pltpu.VMEM((tokens, channels), BF16),
            dma((6,)), dma((groups,)), dma((groups,)),
            pltpu.VMEM(square, F32),
            pltpu.VMEM((8, tokens), F32),
            pltpu.VMEM((2 * tokens + 16, tokens), BF16),
            pltpu.VMEM(square, BF16),
            pltpu.VMEM(square, F32),
            pltpu.VMEM((tokens, WIDTH), jnp.int32),
            pltpu.VMEM(square, F32),
            pltpu.VMEM((chunks, 8, WIDTH), F32),
            pltpu.VMEM(big, F32),
            pltpu.VMEM(big, F32),
            pltpu.VMEM(big, BF16),
            pltpu.VMEM(big, BF16),
            pltpu.VMEM(big, F32),
            pltpu.VMEM(big, F32),
            pltpu.VMEM(big, F32),
            pltpu.VMEM(big, F32),
            pltpu.VMEM(big, BF16),
            pltpu.VMEM(big, BF16),
            pltpu.VMEM(big, BF16),
            pltpu.VMEM(big, BF16),
            pltpu.VMEM(square, F32),
            pltpu.VMEM(square, F32),
            pltpu.VMEM(square, F32),
            pltpu.VMEM(square, F32),
            pltpu.VMEM(square, F32),
            pltpu.VMEM((8, tokens), F32),
            pltpu.VMEM(square, F32),
            pltpu.VMEM(square, F32),
            pltpu.VMEM(square, F32),
            pltpu.VMEM((n, 1, tokens), F32),
            pltpu.VMEM((n * m if n * m <= FLAT else m, 1, tokens), F32),
            dma((1,)), dma((chunks,)), dma((1,)), dma((chunks,)),
            dma((stops,)), dma((stops,)), dma((steps,)), dma((steps,)),
        ],
        compiler_params=pltpu.CompilerParams(
            collective_id=0, has_side_effects=True, vmem_limit_bytes=40 * 2**20),
    )(
        *(pltpu.with_memory_space_constraint(a, pltpu.HBM) for a in (
            dt_raw[0].T, dt_bias[None], a_log[None], d_skip[None],
            x_in[0], b_in[0], c_in[0], cotangent[0]))
    )
    out, gx, gb, gc, gdt, alog, bias, skip = pl.pallas_call(
        functools.partial(place_outputs, 8),
        out_shape=tuple(shape(a.shape, a.dtype) for a in made),
        in_specs=[vmem] * 8,
        out_specs=(hbm,) * 8,
        scratch_shapes=[dma((8,))],
        compiler_params=pltpu.CompilerParams(vmem_limit_bytes=4 * 2**20),
    )(*made)
    return (out[None], gx[None], gb[None], gc[None], gdt.T[None], alog[0], bias[0], skip[0])


def solution(mesh):
    rows = P("batch", "seq", None)
    return jax.shard_map(
        shards,
        mesh=mesh,
        in_specs=(rows, P(), P(), P(), rows, rows, rows, rows),
        out_specs=(rows, rows, rows, rows, rows, P(), P(), P()),
        check_vma=False,
    )
```

```python
import functools

import jax
import jax.numpy as jnp
from jax import lax
from jax.experimental import pallas as pl
from jax.experimental.pallas import tpu as pltpu
from jax.sharding import PartitionSpec as P

HEAD_DIM = 64
WIDTH = 256
F_LAG = 2
B_LAG = 3
UNROLL = 3
FLAT = 64
LOG2E = 1.4426950408889634
F32 = jnp.float32
BF16 = jnp.bfloat16


def mm(a, b):
    return jnp.dot(a, b, preferred_element_type=F32)


def mm_nt(a, b):
    return lax.dot_general(a, b, (((1,), (1,)), ((), ())), preferred_element_type=F32)


def exact(a, b):
    return jnp.dot(a, b, preferred_element_type=F32, precision=lax.Precision.HIGHEST)


def iota(shape, dim):
    return lax.broadcasted_iota(jnp.int32, shape, dim)


def split3(value, heads):
    high = value.astype(BF16).astype(F32)
    rest = value - high
    mid = rest.astype(BF16).astype(F32)
    low = (rest - mid).astype(BF16).astype(F32)
    packed = high + pltpu.roll(mid, heads, 1) + pltpu.roll(low, 2 * heads, 1)
    return packed.astype(BF16)


def kernel(
    n, m, heads, tokens,
    dt_hbm, bias_hbm, alog_hbm, skip_hbm, x_hbm, b_hbm, c_hbm, g_hbm,
    out_ref, gx_ref, gb_ref, gc_ref, gdt_ref, ga_out, gbias_out, gskip_out,
    dt_ref, bias_ref, alog_ref, skip_ref, x_ref, b_ref, c_ref, g_ref,
    in_sem, x_sem, g_sem, pad, prm, pk, apk, vt, kmod, cbm, ms, ee, we, wx, eg, sl, dc, vin, uin,
    fsend, car, bsend, ds,
    cum_ref, ratio, slow, rowa, cola, misc, dcb, gba, gca, reds, redb,
    fs_sem, fr_sem, bs_sem, br_sem, rs_sems, rb_send, rb_recv,
):
    z = lax.axis_index("seq")
    w = lax.axis_index("batch")
    chunks = heads * HEAD_DIM // WIDTH
    per = WIDTH // HEAD_DIM

    unroll = UNROLL if (chunks - 1) % UNROLL == 0 else 1
    groups = 1 + (chunks - 1) // unroll
    small = [
        pltpu.make_async_copy(a, b, in_sem.at[i])
        for i, (a, b) in enumerate((
            (dt_hbm, dt_ref), (bias_hbm, bias_ref), (alog_hbm, alog_ref), (skip_hbm, skip_ref),
            (b_hbm, b_ref), (c_hbm, c_ref)))
    ]

    def fetch(k, first):
        size = WIDTH if first else unroll * WIDTH
        low = 0 if first else pl.multiple_of(WIDTH + (k - 1) * unroll * WIDTH, WIDTH)
        part = pl.ds(low, size)
        return (
            pltpu.make_async_copy(x_hbm.at[:, part], x_ref.at[:, part], x_sem.at[k]),
            pltpu.make_async_copy(g_hbm.at[:, part], g_ref.at[:, part], g_sem.at[k]),
        )

    def fetch_small():
        for copy in small:
            copy.start()
        for copy in fetch(0, True):
            copy.start()

    barrier = pltpu.get_barrier_semaphore()

    def wrap(place, size):
        return jnp.where(place >= size, place - size, place)

    ring_z = [wrap(z + d, n) for d in range(n)]
    ring_w = [wrap(w + d, m) for d in range(m)]

    def other(d):
        return {"seq": ring_z[d // m], "batch": ring_w[d % m]}

    def greet_seq(d, _):
        pl.semaphore_signal(barrier, inc=1, device_id={"seq": lax.rem(z + d, n)},
                            device_id_type=pl.DeviceIdType.MESH)
        return 0

    def greet_batch(d, _):
        pl.semaphore_signal(barrier, inc=1, device_id={"batch": lax.rem(w + d, m)},
                            device_id_type=pl.DeviceIdType.MESH)
        return 0

    flat = n * m <= FLAT
    relay = flat and n > 3
    peers = n * m - 1 if flat else n + m - 2
    edge_peers = 1 if relay else peers
    if not relay:
        fetch_small()
    if relay:
        @pl.when((z == 1) | (z == n - 2))
        def _():
            pl.semaphore_signal(
                barrier, inc=1, device_id={"seq": jnp.where(z == 1, 0, n - 1)},
                device_id_type=pl.DeviceIdType.MESH)

        fetch_small()
        for dw in range(m):
            for inner in range(1, n - 1):

                def greet():
                    pl.semaphore_signal(
                        barrier, inc=1, device_id={"seq": inner, "batch": ring_w[dw]},
                        device_id_type=pl.DeviceIdType.MESH)

                if dw:
                    greet()
                else:
                    pl.when(z != inner)(greet)
    elif flat:
        for d in range(1, n * m):
            pl.semaphore_signal(barrier, inc=1, device_id=other(d),
                                device_id_type=pl.DeviceIdType.MESH)
    else:
        lax.fori_loop(1, n, greet_seq, 0)
        lax.fori_loop(1, m, greet_batch, 0)

    for k in range(1, groups):
        for copy in fetch(k, False):
            copy.start()

    def fcopy(i):
        return pltpu.make_async_remote_copy(
            src_ref=fsend.at[i], dst_ref=car.at[i], send_sem=fs_sem.at[0], recv_sem=fr_sem.at[i],
            device_id={"seq": jnp.minimum(z + 1, n - 1)}, device_id_type=pl.DeviceIdType.MESH)

    def bcopy(i):
        return pltpu.make_async_remote_copy(
            src_ref=bsend.at[i], dst_ref=ds.at[i], send_sem=bs_sem.at[0], recv_sem=br_sem.at[i],
            device_id={"seq": jnp.maximum(z - 1, 0)}, device_id_type=pl.DeviceIdType.MESH)

    pad[...] = jnp.zeros_like(pad)
    prm[...] = jnp.zeros_like(prm)
    for copy in small:
        copy.wait()
    pad[0:heads, :] = dt_ref[...]
    prm[0:1, :heads] = bias_ref[...]
    prm[1:2, :heads] = alog_ref[...]
    prm[2:3, :heads] = skip_ref[...]
    square = (tokens, tokens)
    is_head = iota(square, 1) < heads
    raw = pad[...].T + prm[0:1, :]
    step = jnp.maximum(raw, 0.0) + jnp.log1p(jnp.exp(-jnp.abs(raw)))
    rate = jnp.exp(prm[1:2, :])
    decay = jnp.where(is_head, -rate * step, 0.0)
    causal = iota(square, 0) >= iota(square, 1)
    slope = 1.0 / (1.0 + jnp.exp(-raw))
    cum = exact(jnp.where(causal, 1.0, 0.0), decay)
    last = cum[tokens - 1 : tokens, :]
    pk[0:tokens, :] = split3(jnp.where(is_head, jnp.exp(cum), 0.0), heads)
    pk[tokens : 2 * tokens, :] = split3(
        jnp.where(is_head, jnp.exp(last - cum) * step, 0.0), heads)
    head_row = is_head[0:1, :]
    factor = jnp.where(head_row, jnp.exp(last.astype(BF16).astype(F32)), 0.0)
    row16 = iota((16, tokens), 0)
    pk[2 * tokens : 2 * tokens + 16, :] = split3(
        jnp.where(row16 == 0, prm[2:3, :], 0.0) + jnp.where(row16 == 1, factor, 0.0), heads)
    k = iota((tokens, WIDTH), 0)
    kmod[...] = k - jnp.where(k >= heads, heads, 0) - jnp.where(k >= 2 * heads, heads, 0)
    b16 = b_ref[...]
    c16 = c_ref[...]
    bt = b16.astype(F32).T.astype(BF16)
    ct = c16.astype(F32).T.astype(BF16)

    edge = (z == 0) | (z == n - 1)
    place = z * m + w

    def cols(i):
        return pl.ds(pl.multiple_of(i * WIDTH, WIDTH), WIDTH)

    def state(i):
        group = lax.shift_right_logical(iota((tokens, WIDTH), 1), 6)
        spread = jnp.where(kmod[...] - group == i * per, 1.0, 0.0).astype(BF16)
        wide = mm(pk[...], spread)
        yield
        ee[i] = wide[0:tokens]
        we[i] = wide[tokens : 2 * tokens]
        ms[i] = wide[2 * tokens : 2 * tokens + 8]
        wx_i = (x_ref[:, cols(i)].astype(F32) * wide[tokens : 2 * tokens]).astype(BF16)
        eg_i = (g_ref[:, cols(i)].astype(F32) * wide[0:tokens]).astype(BF16)
        wx[i] = wx_i
        eg[i] = eg_i
        yield
        sl_i = mm(bt, wx_i)
        dc_i = mm(ct, eg_i)
        yield
        sl[i] = sl_i
        dc[i] = dc_i

    def together(*stages):
        stages = list(stages)
        while stages:
            stages = [stage for stage in stages if next(stage, 0) is None]

    def announce(i):
        @pl.when(z == 0)
        def _():
            car[i] = jnp.zeros((tokens, WIDTH), BF16)
            fsend[i] = sl[i].astype(BF16)
            fcopy(i).start()

        @pl.when(z == n - 1)
        def _():
            ds[i] = jnp.zeros((tokens, WIDTH), BF16)
            bsend[i] = dc[i].astype(BF16)
            bcopy(i).start()

    def states(k, _):
        for copy in fetch(1 + k, False):
            copy.wait()
        together(*(state(1 + k * unroll + u) for u in range(unroll)))
        for u in range(unroll):
            announce(1 + k * unroll + u)
        return 0

    for copy in fetch(0, True):
        copy.wait()
    together(state(0))

    @pl.when(edge)
    def _():
        pl.semaphore_wait(barrier, edge_peers)

    announce(0)
    lax.fori_loop(0, (chunks - 1) // unroll, states, 0)

    cum_ref[...] = cum
    ratio[...] = slope / step
    slow[...] = rate * exact(jnp.where(causal, 1.0, 0.0), slope)
    cum2 = cum * LOG2E
    apk[...] = split3(cum2, heads)
    vt[...] = (cum2 - jnp.log(step) * LOG2E).T
    cbm[...] = jnp.where(causal, mm(c16, bt), 0.0)
    for acc in (rowa, cola, misc, dcb, gba, gca):
        acc[...] = jnp.zeros_like(acc)

    @pl.when(jnp.logical_not(edge))
    def _():
        pl.semaphore_wait(barrier, peers)


    def to_heads(value, i):
        group = lax.shift_right_logical(iota((WIDTH, tokens), 0), 6)
        gather = jnp.where(iota((WIDTH, tokens), 1) - group == i * per, 1.0, 0.0).astype(BF16)
        high = value.astype(BF16)
        low = (value - high.astype(F32)).astype(BF16)
        return mm(high, gather) + mm(low, gather)

    def within(i):
        lane = iota(square, 1)
        left = jnp.where(lane < HEAD_DIM, 1.0, 0.0).astype(BF16)
        right = jnp.where(lane < HEAD_DIM, 0.0, 1.0).astype(BF16)
        second = jnp.where(iota((tokens, 2 * tokens), 1) < tokens, 0, 1)
        table = kmod[:, 0:1] - second
        count = WIDTH // 128
        heads_of = [i * per + 2 * q for q in range(count)]
        pairs = [pl.ds(pl.multiple_of(i * WIDTH + q * 128, 128), 128) for q in range(count)]
        xqs = [x_ref[:, pair] for pair in pairs]
        gqs = [g_ref[:, pair] for pair in pairs]
        xss = [jnp.concatenate([xq * left, xq * right], axis=0) for xq in xqs]
        gss = [jnp.concatenate([gq * left, gq * right], axis=0) for gq in gqs]
        logs = [
            mm(apk[...], jnp.where(table == head, 1.0, 0.0).astype(BF16)) for head in heads_of]
        gates = []
        for head, log in zip(heads_of, logs):
            v_row = jnp.concatenate([vt[pl.ds(head, 1), :], vt[pl.ds(head + 1, 1), :]], axis=1)
            gates.append(jnp.exp2(jnp.minimum(log - v_row, 100.0)))
        cb = cbm[...]
        scores = [
            [(gate[:, h * tokens : (h + 1) * tokens] * cb).astype(BF16) for h in range(2)]
            for gate in gates]
        turned = [jnp.concatenate([part.T for part in both], axis=1) for both in scores]
        grads = [mm_nt(gq, xs) * gate for gq, xs, gate in zip(gqs, xss, gates)]
        for q in range(count):
            vin[i, :, q * 128 : (q + 1) * 128] = mm(jnp.concatenate(scores[q], axis=1), xss[q])
            uin[i, :, q * 128 : (q + 1) * 128] = mm(turned[q], gss[q])
        total = grads[0][:, :tokens] + grads[0][:, tokens:]
        for grad in grads[1:]:
            total = total + grad[:, :tokens] + grad[:, tokens:]
        dcb[...] += total

    def forward(i):
        state_in = car[i]
        inter = mm(c16, state_in)
        to_c = mm_nt(eg[i], state_in)
        yield
        x_i = x_ref[:, cols(i)].astype(F32)
        v = vin[i] + ee[i] * inter
        out_ref[:, cols(i)] = (v + ms[i, 0:1, :] * x_i).astype(BF16)
        share = g_ref[:, cols(i)].astype(F32) * v
        yield
        share = to_heads(share, i)
        yield
        rowa[...] += share
        gca[...] += to_c

    def backward(i):
        state_in = ds[i]
        from_state = mm(b16, state_in)
        to_b = mm_nt(wx[i], state_in)
        yield
        g_i = g_ref[:, cols(i)].astype(F32)
        u = uin[i]
        gx_ref[:, cols(i)] = (u + we[i] * from_state + ms[i, 0:1, :] * g_i).astype(BF16)
        share = x_ref[:, cols(i)].astype(F32) * u + wx[i].astype(F32) * from_state
        yield
        share = to_heads(share, i)
        yield
        cola[...] += share
        gba[...] += to_b

    def sums(i):
        onward = ms[i, 1:2, :] * car[i].astype(F32) + sl[i]
        d_last = jnp.sum(onward * ds[i].astype(F32), axis=0, keepdims=True)
        d_skip = jnp.sum(
            g_ref[:, cols(i)].astype(F32) * x_ref[:, cols(i)].astype(F32), axis=0, keepdims=True)
        row = iota((8, WIDTH), 0)
        both = jnp.where(row == 0, d_last, 0.0) + jnp.where(row == 1, d_skip, 0.0)
        yield
        both = to_heads(both, i)
        yield
        misc[...] += both

    cases = set()
    for row in range(n):
        for j in range(chunks + max(F_LAG, B_LAG) * max(n - 2, 0)):
            f = j - F_LAG * max(row - 1, 0)
            b = j - B_LAG * max(n - 2 - row, 0)
            marks = (0 <= f < chunks, 0 <= b < chunks, 0 <= min(f, b) < chunks)
            cases.add(sum(1 << k for k, mark in enumerate(marks) if mark))
    cases = sorted(cases - {0})

    def advance(j, _):
        f = j - F_LAG * jnp.maximum(z - 1, 0)
        b = j - B_LAG * jnp.maximum(n - 2 - z, 0)
        both = jnp.minimum(f, b)
        f_on = (f >= 0) & (f < chunks)
        b_on = (b >= 0) & (b < chunks)

        @pl.when(f_on & (z > 0))
        def _():
            fcopy(f).wait_recv()
            fsend[f] = (ms[f, 1:2, :] * car[f].astype(F32) + sl[f]).astype(BF16)

        @pl.when(f_on & (z > 0) & (z < n - 1))
        def _():
            fcopy(f).start()

        @pl.when(j < chunks)
        def _():
            within(j)

        @pl.when(b_on & (z < n - 1))
        def _():
            bcopy(b).wait_recv()

        @pl.when(b_on & (z < n - 1) & (z > 0))
        def _():
            bsend[b] = (ms[b, 1:2, :] * ds[b].astype(F32) + dc[b]).astype(BF16)
            bcopy(b).start()

        kind = (
            jnp.where(f_on, 1, 0) + jnp.where(b_on, 2, 0)
            + jnp.where((both >= 0) & (both < chunks), 4, 0)
        )
        for case in cases:

            @pl.when(kind == case)
            def _():
                together(*(
                    part(i) for bit, part, i in ((1, forward, f), (2, backward, b), (4, sums, both))
                    if case & bit))

        return 0

    lax.fori_loop(0, chunks + max(F_LAG, B_LAG) * max(n - 2, 0), advance, 0)

    d_cum = rowa[...] - cola[...]
    d_cum = d_cum + jnp.where(iota(square, 0) == tokens - 1, misc[0:1, :], 0.0)
    grad_a = jnp.sum(d_cum * cum_ref[...], axis=0, keepdims=True)
    grad_bias = jnp.sum(cola[...] * ratio[...] - d_cum * slow[...], axis=0, keepdims=True)

    def turn(row, by):
        return pltpu.roll(jnp.broadcast_to(row, (8, tokens)), by, 1)[0:1, :]

    def per_head(row):
        return jnp.where(head_row, row, 0.0)

    mine = (
        per_head(grad_a) + turn(per_head(grad_bias), heads)
        + turn(per_head(misc[1:2, :]), 2 * heads)
    )

    def seq_copy(d):
        return pltpu.make_async_remote_copy(
            src_ref=reds.at[z], dst_ref=reds.at[z], send_sem=rs_sems.at[d - 1],
            recv_sem=rs_sems.at[n - 1 + d - 1], device_id={"seq": lax.rem(z + d, n)},
            device_id_type=pl.DeviceIdType.MESH)

    def batch_copy(d):
        return pltpu.make_async_remote_copy(
            src_ref=redb.at[w], dst_ref=redb.at[w], send_sem=rb_send.at[d - 1],
            recv_sem=rb_recv.at[d - 1], device_id={"batch": lax.rem(w + d, m)},
            device_id_type=pl.DeviceIdType.MESH)

    def flat_copy(to):
        return pltpu.make_async_remote_copy(
            src_ref=redb.at[place], dst_ref=redb.at[place], send_sem=rb_send.at[0],
            recv_sem=rb_recv.at[0],
            device_id={"seq": jnp.int32(to // m), "batch": jnp.int32(to % m)},
            device_id_type=pl.DeviceIdType.MESH)

    def flat_wait(sem):
        rows = redb.at[pl.ds(0, n * m - 1)]
        pltpu.make_async_copy(rows, rows, sem).wait()

    def start(copy):
        return lambda d, _: (copy(d).start(), 0)[1]

    def finish(copy):
        return lambda d, _: (copy(d).wait(), 0)[1]

    if flat:
        redb[place] = mine
        for to in range(n * m):
            pl.when(place != to)(lambda: flat_copy(to).start())
    else:
        reds[z] = mine
        lax.fori_loop(1, n, start(seq_copy), 0)
    later = iota(square, 0) <= iota(square, 1)
    d_decay = exact(jnp.where(later, 1.0, 0.0), d_cum)
    d_raw = cola[...] * ratio[...] - rate * slope * d_decay
    gdt_ref[...] = d_raw.T[0:heads, :]
    d_cb = jnp.where(causal, dcb[...], 0.0)
    gc_ref[...] = (gca[...] + mm(d_cb.astype(BF16), b16)).astype(BF16)
    gb_ref[...] = (gba[...] + mm(d_cb.T.astype(BF16), c16)).astype(BF16)
    if not flat:
        lax.fori_loop(1, n, finish(seq_copy), 0)
        redb[w] = lax.fori_loop(0, n, lambda i, t: t + reds[i], jnp.zeros((1, tokens), F32))
        lax.fori_loop(1, m, start(batch_copy), 0)

    @pl.when(z < n - 1)
    def _():
        pltpu.make_async_copy(fsend, fsend, fs_sem.at[0]).wait()

    @pl.when(z > 0)
    def _():
        pltpu.make_async_copy(bsend, bsend, bs_sem.at[0]).wait()

    if flat:
        flat_wait(rb_send.at[0])
        flat_wait(rb_recv.at[0])
    else:
        lax.fori_loop(1, m, finish(batch_copy), 0)
    total = jnp.sum(redb[...], axis=0)
    ga_out[...] = total[:, :heads]
    gbias_out[...] = turn(total, tokens - heads)[:, :heads]
    gskip_out[...] = turn(total, tokens - 2 * heads)[:, :heads]


def place_outputs(count, *refs):
    sems = refs[2 * count]
    copies = [
        pltpu.make_async_copy(refs[i], refs[count + i], sems.at[i]) for i in range(count)
    ]
    for copy in copies:
        copy.start()
    for copy in copies:
        copy.wait()


def shards(dt_raw, dt_bias, a_log, d_skip, x_in, b_in, c_in, cotangent):
    n, m = lax.axis_size("seq"), lax.axis_size("batch")
    _, tokens, heads = dt_raw.shape
    channels = x_in.shape[2]
    state = b_in.shape[2]
    chunks = channels // WIDTH
    steps = 1 if n * m <= FLAT else m - 1
    stops = 1 if n * m <= FLAT else 2 * (n - 1)
    groups = 1 + (chunks - 1) // (UNROLL if (chunks - 1) % UNROLL == 0 else 1)
    big = (chunks, tokens, WIDTH)
    square = (tokens, tokens)
    vmem = pl.BlockSpec(memory_space=pltpu.VMEM)
    hbm = pl.BlockSpec(memory_space=pltpu.HBM)
    dma = pltpu.SemaphoreType.DMA
    shape = jax.ShapeDtypeStruct
    made = pl.pallas_call(
        functools.partial(kernel, n, m, heads, tokens),
        out_shape=(
            shape((tokens, channels), BF16),
            shape((tokens, channels), BF16),
            shape((tokens, state), BF16),
            shape((tokens, state), BF16),
            shape((heads, tokens), F32),
        ) + (shape((1, heads), F32),) * 3,
        in_specs=[hbm] * 8,
        out_specs=(vmem,) * 8,
        scratch_shapes=[
            pltpu.VMEM((heads, tokens), F32),
            pltpu.VMEM((1, heads), F32),
            pltpu.VMEM((1, heads), F32),
            pltpu.VMEM((1, heads), F32),
            pltpu.VMEM((tokens, channels), BF16),
            pltpu.VMEM((tokens, state), BF16),
            pltpu.VMEM((tokens, state), BF16),
            pltpu.VMEM((tokens, channels), BF16),
            dma((6,)), dma((groups,)), dma((groups,)),
            pltpu.VMEM(square, F32),
            pltpu.VMEM((8, tokens), F32),
            pltpu.VMEM((2 * tokens + 16, tokens), BF16),
            pltpu.VMEM(square, BF16),
            pltpu.VMEM(square, F32),
            pltpu.VMEM((tokens, WIDTH), jnp.int32),
            pltpu.VMEM(square, F32),
            pltpu.VMEM((chunks, 8, WIDTH), F32),
            pltpu.VMEM(big, F32),
            pltpu.VMEM(big, F32),
            pltpu.VMEM(big, BF16),
            pltpu.VMEM(big, BF16),
            pltpu.VMEM(big, F32),
            pltpu.VMEM(big, F32),
            pltpu.VMEM(big, F32),
            pltpu.VMEM(big, F32),
            pltpu.VMEM(big, BF16),
            pltpu.VMEM(big, BF16),
            pltpu.VMEM(big, BF16),
            pltpu.VMEM(big, BF16),
            pltpu.VMEM(square, F32),
            pltpu.VMEM(square, F32),
            pltpu.VMEM(square, F32),
            pltpu.VMEM(square, F32),
            pltpu.VMEM(square, F32),
            pltpu.VMEM((8, tokens), F32),
            pltpu.VMEM(square, F32),
            pltpu.VMEM(square, F32),
            pltpu.VMEM(square, F32),
            pltpu.VMEM((n, 1, tokens), F32),
            pltpu.VMEM((n * m if n * m <= FLAT else m, 1, tokens), F32),
            dma((1,)), dma((chunks,)), dma((1,)), dma((chunks,)),
            dma((stops,)), dma((steps,)), dma((steps,)),
        ],
        compiler_params=pltpu.CompilerParams(
            collective_id=0, has_side_effects=True, vmem_limit_bytes=40 * 2**20),
    )(
        *(pltpu.with_memory_space_constraint(a, pltpu.HBM) for a in (
            dt_raw[0].T, dt_bias[None], a_log[None], d_skip[None],
            x_in[0], b_in[0], c_in[0], cotangent[0]))
    )
    out, gx, gb, gc, gdt, alog, bias, skip = pl.pallas_call(
        functools.partial(place_outputs, 8),
        out_shape=tuple(shape(a.shape, a.dtype) for a in made),
        in_specs=[vmem] * 8,
        out_specs=(hbm,) * 8,
        scratch_shapes=[dma((8,))],
        compiler_params=pltpu.CompilerParams(vmem_limit_bytes=4 * 2**20),
    )(*made)
    return (out[None], gx[None], gb[None], gc[None], gdt.T[None], alog[0], bias[0], skip[0])


def solution(mesh):
    rows = P("batch", "seq", None)
    return jax.shard_map(
        shards,
        mesh=mesh,
        in_specs=(rows, P(), P(), P(), rows, rows, rows, rows),
        out_specs=(rows, rows, rows, rows, rows, P(), P(), P()),
        check_vma=False,
    )
```

```python
import functools

import jax
import jax.numpy as jnp
from jax import lax
from jax.experimental import pallas as pl
from jax.experimental.pallas import tpu as pltpu
from jax.sharding import PartitionSpec as P

HEAD_DIM = 64
WIDTH = 256
F_LAG = 2
B_LAG = 3
UNROLL = 3
FLAT = 64
LOG2E = 1.4426950408889634
F32 = jnp.float32
BF16 = jnp.bfloat16


def mm(a, b):
    return jnp.dot(a, b, preferred_element_type=F32)


def mm_nt(a, b):
    return lax.dot_general(a, b, (((1,), (1,)), ((), ())), preferred_element_type=F32)


def exact(a, b):
    return jnp.dot(a, b, preferred_element_type=F32, precision=lax.Precision.HIGHEST)


def iota(shape, dim):
    return lax.broadcasted_iota(jnp.int32, shape, dim)


def split3(value, heads):
    high = value.astype(BF16).astype(F32)
    rest = value - high
    mid = rest.astype(BF16).astype(F32)
    low = (rest - mid).astype(BF16).astype(F32)
    packed = high + pltpu.roll(mid, heads, 1) + pltpu.roll(low, 2 * heads, 1)
    return packed.astype(BF16)


def kernel(
    n, m, heads, tokens,
    dt_hbm, bias_hbm, alog_hbm, skip_hbm, x_hbm, b_hbm, c_hbm, g_hbm,
    out_ref, gx_ref, gb_ref, gc_ref, gdt_ref, ga_out, gbias_out, gskip_out,
    dt_ref, bias_ref, alog_ref, skip_ref, x_ref, b_ref, c_ref, g_ref,
    in_sem, x_sem, g_sem, pad, prm, pk, apk, vt, kmod, cbm, ms, ee, we, wx, eg, sl, dc, vin, uin,
    fsend, car, bsend, ds,
    cum_ref, ratio, slow, rowa, cola, misc, dcb, gba, gca, reds, redb,
    fs_sem, fr_sem, bs_sem, br_sem, rs_sems, rb_send, rb_recv,
):
    z = lax.axis_index("seq")
    w = lax.axis_index("batch")
    chunks = heads * HEAD_DIM // WIDTH
    per = WIDTH // HEAD_DIM

    unroll = UNROLL if (chunks - 1) % UNROLL == 0 else 1
    groups = 1 + (chunks - 1) // unroll
    small = [
        pltpu.make_async_copy(a, b, in_sem.at[i])
        for i, (a, b) in enumerate((
            (dt_hbm, dt_ref), (bias_hbm, bias_ref), (alog_hbm, alog_ref), (skip_hbm, skip_ref),
            (b_hbm, b_ref), (c_hbm, c_ref)))
    ]

    def fetch(k, first):
        size = WIDTH if first else unroll * WIDTH
        low = 0 if first else pl.multiple_of(WIDTH + (k - 1) * unroll * WIDTH, WIDTH)
        part = pl.ds(low, size)
        return (
            pltpu.make_async_copy(x_hbm.at[:, part], x_ref.at[:, part], x_sem.at[k]),
            pltpu.make_async_copy(g_hbm.at[:, part], g_ref.at[:, part], g_sem.at[k]),
        )

    def fetch_small():
        for copy in small:
            copy.start()
        for copy in fetch(0, True):
            copy.start()

    barrier = pltpu.get_barrier_semaphore()

    def wrap(place, size):
        return jnp.where(place >= size, place - size, place)

    ring_z = [wrap(z + d, n) for d in range(n)]
    ring_w = [wrap(w + d, m) for d in range(m)]

    def other(d):
        return {"seq": ring_z[d // m], "batch": ring_w[d % m]}

    def greet_seq(d, _):
        pl.semaphore_signal(barrier, inc=1, device_id={"seq": lax.rem(z + d, n)},
                            device_id_type=pl.DeviceIdType.MESH)
        return 0

    def greet_batch(d, _):
        pl.semaphore_signal(barrier, inc=1, device_id={"batch": lax.rem(w + d, m)},
                            device_id_type=pl.DeviceIdType.MESH)
        return 0

    flat = n * m <= FLAT
    relay = flat and n > 3
    peers = n * m - 1 if flat else n + m - 2
    edge_peers = 1 if relay else peers
    if not relay:
        fetch_small()
    if relay:
        @pl.when((z == 1) | (z == n - 2))
        def _():
            pl.semaphore_signal(
                barrier, inc=1, device_id={"seq": jnp.where(z == 1, 0, n - 1)},
                device_id_type=pl.DeviceIdType.MESH)

        fetch_small()
        for dw in range(m):
            for inner in range(1, n - 1):

                def greet():
                    pl.semaphore_signal(
                        barrier, inc=1, device_id={"seq": inner, "batch": ring_w[dw]},
                        device_id_type=pl.DeviceIdType.MESH)

                if dw:
                    greet()
                else:
                    pl.when(z != inner)(greet)
    elif flat:
        for d in range(1, n * m):
            pl.semaphore_signal(barrier, inc=1, device_id=other(d),
                                device_id_type=pl.DeviceIdType.MESH)
    else:
        lax.fori_loop(1, n, greet_seq, 0)
        lax.fori_loop(1, m, greet_batch, 0)

    for k in range(1, groups):
        for copy in fetch(k, False):
            copy.start()

    def fcopy(i):
        return pltpu.make_async_remote_copy(
            src_ref=fsend.at[i], dst_ref=car.at[i], send_sem=fs_sem.at[0], recv_sem=fr_sem.at[i],
            device_id={"seq": jnp.minimum(z + 1, n - 1)}, device_id_type=pl.DeviceIdType.MESH)

    def bcopy(i):
        return pltpu.make_async_remote_copy(
            src_ref=bsend.at[i], dst_ref=ds.at[i], send_sem=bs_sem.at[0], recv_sem=br_sem.at[i],
            device_id={"seq": jnp.maximum(z - 1, 0)}, device_id_type=pl.DeviceIdType.MESH)

    pad[...] = jnp.zeros_like(pad)
    prm[...] = jnp.zeros_like(prm)
    for copy in small:
        copy.wait()
    pad[0:heads, :] = dt_ref[...]
    prm[0:1, :heads] = bias_ref[...]
    prm[1:2, :heads] = alog_ref[...]
    prm[2:3, :heads] = skip_ref[...]
    square = (tokens, tokens)
    is_head = iota(square, 1) < heads
    raw = pad[...].T + prm[0:1, :]
    step = jnp.maximum(raw, 0.0) + jnp.log1p(jnp.exp(-jnp.abs(raw)))
    rate = jnp.exp(prm[1:2, :])
    decay = jnp.where(is_head, -rate * step, 0.0)
    causal = iota(square, 0) >= iota(square, 1)
    slope = 1.0 / (1.0 + jnp.exp(-raw))
    cum = exact(jnp.where(causal, 1.0, 0.0), decay)
    last = cum[tokens - 1 : tokens, :]
    pk[0:tokens, :] = split3(jnp.where(is_head, jnp.exp(cum), 0.0), heads)
    pk[tokens : 2 * tokens, :] = split3(
        jnp.where(is_head, jnp.exp(last - cum) * step, 0.0), heads)
    head_row = is_head[0:1, :]
    factor = jnp.where(head_row, jnp.exp(last.astype(BF16).astype(F32)), 0.0)
    row16 = iota((16, tokens), 0)
    pk[2 * tokens : 2 * tokens + 16, :] = split3(
        jnp.where(row16 == 0, prm[2:3, :], 0.0) + jnp.where(row16 == 1, factor, 0.0), heads)
    k = iota((tokens, WIDTH), 0)
    kmod[...] = k - jnp.where(k >= heads, heads, 0) - jnp.where(k >= 2 * heads, heads, 0)
    b16 = b_ref[...]
    c16 = c_ref[...]
    bt = b16.astype(F32).T.astype(BF16)
    ct = c16.astype(F32).T.astype(BF16)

    edge = (z == 0) | (z == n - 1)
    place = z * m + w

    def cols(i):
        return pl.ds(pl.multiple_of(i * WIDTH, WIDTH), WIDTH)

    def state(i):
        group = lax.shift_right_logical(iota((tokens, WIDTH), 1), 6)
        spread = jnp.where(kmod[...] - group == i * per, 1.0, 0.0).astype(BF16)
        wide = mm(pk[...], spread)
        yield
        ee[i] = wide[0:tokens]
        we[i] = wide[tokens : 2 * tokens]
        ms[i] = wide[2 * tokens : 2 * tokens + 8]
        wx_i = (x_ref[:, cols(i)].astype(F32) * wide[tokens : 2 * tokens]).astype(BF16)
        eg_i = (g_ref[:, cols(i)].astype(F32) * wide[0:tokens]).astype(BF16)
        wx[i] = wx_i
        eg[i] = eg_i
        yield
        sl_i = mm(bt, wx_i)
        dc_i = mm(ct, eg_i)
        yield
        sl[i] = sl_i
        dc[i] = dc_i

    def together(*stages):
        stages = list(stages)
        while stages:
            stages = [stage for stage in stages if next(stage, 0) is None]

    def announce(i):
        @pl.when(z == 0)
        def _():
            car[i] = jnp.zeros((tokens, WIDTH), BF16)
            fsend[i] = sl[i].astype(BF16)
            fcopy(i).start()

        @pl.when(z == n - 1)
        def _():
            ds[i] = jnp.zeros((tokens, WIDTH), BF16)
            bsend[i] = dc[i].astype(BF16)
            bcopy(i).start()

    def states(k, _):
        for copy in fetch(1 + k, False):
            copy.wait()
        together(*(state(1 + k * unroll + u) for u in range(unroll)))
        for u in range(unroll):
            announce(1 + k * unroll + u)
        return 0

    for copy in fetch(0, True):
        copy.wait()
    together(state(0))

    @pl.when(edge)
    def _():
        pl.semaphore_wait(barrier, edge_peers)

    announce(0)
    lax.fori_loop(0, (chunks - 1) // unroll, states, 0)

    cum_ref[...] = cum
    ratio[...] = slope / step
    slow[...] = rate * exact(jnp.where(causal, 1.0, 0.0), slope)
    cum2 = cum * LOG2E
    apk[...] = split3(cum2, heads)
    vt[...] = (cum2 - jnp.log(step) * LOG2E).T
    cbm[...] = jnp.where(causal, mm(c16, bt), 0.0)
    for acc in (rowa, cola, misc, dcb, gba, gca):
        acc[...] = jnp.zeros_like(acc)

    @pl.when(jnp.logical_not(edge))
    def _():
        pl.semaphore_wait(barrier, peers)


    def to_heads(value, i):
        group = lax.shift_right_logical(iota((WIDTH, tokens), 0), 6)
        gather = jnp.where(iota((WIDTH, tokens), 1) - group == i * per, 1.0, 0.0).astype(BF16)
        high = value.astype(BF16)
        low = (value - high.astype(F32)).astype(BF16)
        return mm(high, gather) + mm(low, gather)

    def within(i):
        lane = iota(square, 1)
        left = jnp.where(lane < HEAD_DIM, 1.0, 0.0).astype(BF16)
        right = jnp.where(lane < HEAD_DIM, 0.0, 1.0).astype(BF16)
        second = jnp.where(iota((tokens, 2 * tokens), 1) < tokens, 0, 1)
        table = kmod[:, 0:1] - second
        count = WIDTH // 128
        heads_of = [i * per + 2 * q for q in range(count)]
        pairs = [pl.ds(pl.multiple_of(i * WIDTH + q * 128, 128), 128) for q in range(count)]
        xqs = [x_ref[:, pair] for pair in pairs]
        gqs = [g_ref[:, pair] for pair in pairs]
        xss = [jnp.concatenate([xq * left, xq * right], axis=0) for xq in xqs]
        gss = [jnp.concatenate([gq * left, gq * right], axis=0) for gq in gqs]
        logs = [
            mm(apk[...], jnp.where(table == head, 1.0, 0.0).astype(BF16)) for head in heads_of]
        gates = []
        for head, log in zip(heads_of, logs):
            v_row = jnp.concatenate([vt[pl.ds(head, 1), :], vt[pl.ds(head + 1, 1), :]], axis=1)
            gates.append(jnp.exp2(jnp.minimum(log - v_row, 100.0)))
        cb = cbm[...]
        scores = [
            [(gate[:, h * tokens : (h + 1) * tokens] * cb).astype(BF16) for h in range(2)]
            for gate in gates]
        turned = [jnp.concatenate([part.T for part in both], axis=1) for both in scores]
        grads = [mm_nt(gq, xs) * gate for gq, xs, gate in zip(gqs, xss, gates)]
        for q in range(count):
            vin[i, :, q * 128 : (q + 1) * 128] = mm(jnp.concatenate(scores[q], axis=1), xss[q])
            uin[i, :, q * 128 : (q + 1) * 128] = mm(turned[q], gss[q])
        total = grads[0][:, :tokens] + grads[0][:, tokens:]
        for grad in grads[1:]:
            total = total + grad[:, :tokens] + grad[:, tokens:]
        dcb[...] += total

    def forward(i):
        state_in = car[i]
        inter = mm(c16, state_in)
        to_c = mm_nt(eg[i], state_in)
        yield
        x_i = x_ref[:, cols(i)].astype(F32)
        v = vin[i] + ee[i] * inter
        out_ref[:, cols(i)] = (v + ms[i, 0:1, :] * x_i).astype(BF16)
        share = g_ref[:, cols(i)].astype(F32) * v
        yield
        share = to_heads(share, i)
        yield
        rowa[...] += share
        gca[...] += to_c

    def backward(i):
        state_in = ds[i]
        from_state = mm(b16, state_in)
        to_b = mm_nt(wx[i], state_in)
        yield
        g_i = g_ref[:, cols(i)].astype(F32)
        u = uin[i]
        gx_ref[:, cols(i)] = (u + we[i] * from_state + ms[i, 0:1, :] * g_i).astype(BF16)
        share = x_ref[:, cols(i)].astype(F32) * u + wx[i].astype(F32) * from_state
        yield
        share = to_heads(share, i)
        yield
        cola[...] += share
        gba[...] += to_b

    def sums(i):
        onward = ms[i, 1:2, :] * car[i].astype(F32) + sl[i]
        d_last = jnp.sum(onward * ds[i].astype(F32), axis=0, keepdims=True)
        d_skip = jnp.sum(
            g_ref[:, cols(i)].astype(F32) * x_ref[:, cols(i)].astype(F32), axis=0, keepdims=True)
        row = iota((8, WIDTH), 0)
        both = jnp.where(row == 0, d_last, 0.0) + jnp.where(row == 1, d_skip, 0.0)
        yield
        both = to_heads(both, i)
        yield
        misc[...] += both

    cases = set()
    for row in range(n):
        for j in range(chunks + max(F_LAG, B_LAG) * max(n - 2, 0)):
            f = j - F_LAG * max(row - 1, 0)
            b = j - B_LAG * max(n - 2 - row, 0)
            marks = (0 <= f < chunks, 0 <= b < chunks, 0 <= min(f, b) < chunks)
            cases.add(sum(1 << k for k, mark in enumerate(marks) if mark))
    cases = sorted(cases - {0})

    def advance(j, _):
        f = j - F_LAG * jnp.maximum(z - 1, 0)
        b = j - B_LAG * jnp.maximum(n - 2 - z, 0)
        both = jnp.minimum(f, b)
        f_on = (f >= 0) & (f < chunks)
        b_on = (b >= 0) & (b < chunks)

        @pl.when(f_on & (z > 0))
        def _():
            fcopy(f).wait_recv()
            fsend[f] = (ms[f, 1:2, :] * car[f].astype(F32) + sl[f]).astype(BF16)

        @pl.when(f_on & (z > 0) & (z < n - 1))
        def _():
            fcopy(f).start()

        @pl.when(j < chunks)
        def _():
            within(j)

        @pl.when(b_on & (z < n - 1))
        def _():
            bcopy(b).wait_recv()

        @pl.when(b_on & (z < n - 1) & (z > 0))
        def _():
            bsend[b] = (ms[b, 1:2, :] * ds[b].astype(F32) + dc[b]).astype(BF16)
            bcopy(b).start()

        kind = (
            jnp.where(f_on, 1, 0) + jnp.where(b_on, 2, 0)
            + jnp.where((both >= 0) & (both < chunks), 4, 0)
        )
        for case in cases:

            @pl.when(kind == case)
            def _():
                together(*(
                    part(i) for bit, part, i in ((1, forward, f), (2, backward, b), (4, sums, both))
                    if case & bit))

        return 0

    lax.fori_loop(0, chunks + max(F_LAG, B_LAG) * max(n - 2, 0), advance, 0)

    d_cum = rowa[...] - cola[...]
    d_cum = d_cum + jnp.where(iota(square, 0) == tokens - 1, misc[0:1, :], 0.0)
    grad_a = jnp.sum(d_cum * cum_ref[...], axis=0, keepdims=True)
    grad_bias = jnp.sum(cola[...] * ratio[...] - d_cum * slow[...], axis=0, keepdims=True)

    def turn(row, by):
        return pltpu.roll(jnp.broadcast_to(row, (8, tokens)), by, 1)[0:1, :]

    def per_head(row):
        return jnp.where(head_row, row, 0.0)

    mine = (
        per_head(grad_a) + turn(per_head(grad_bias), heads)
        + turn(per_head(misc[1:2, :]), 2 * heads)
    )

    def seq_copy(d):
        return pltpu.make_async_remote_copy(
            src_ref=reds.at[z], dst_ref=reds.at[z], send_sem=rs_sems.at[d - 1],
            recv_sem=rs_sems.at[n - 1 + d - 1], device_id={"seq": lax.rem(z + d, n)},
            device_id_type=pl.DeviceIdType.MESH)

    def batch_copy(d):
        return pltpu.make_async_remote_copy(
            src_ref=redb.at[w], dst_ref=redb.at[w], send_sem=rb_send.at[d - 1],
            recv_sem=rb_recv.at[d - 1], device_id={"batch": lax.rem(w + d, m)},
            device_id_type=pl.DeviceIdType.MESH)

    def flat_copy(to):
        return pltpu.make_async_remote_copy(
            src_ref=redb.at[place], dst_ref=redb.at[place], send_sem=rb_send.at[0],
            recv_sem=rb_recv.at[0],
            device_id={"seq": jnp.int32(to // m), "batch": jnp.int32(to % m)},
            device_id_type=pl.DeviceIdType.MESH)

    def flat_wait(sem):
        rows = redb.at[pl.ds(0, n * m - 1)]
        pltpu.make_async_copy(rows, rows, sem).wait()

    def start(copy):
        return lambda d, _: (copy(d).start(), 0)[1]

    def finish(copy):
        return lambda d, _: (copy(d).wait(), 0)[1]

    if flat:
        redb[place] = mine
        for to in range(n * m):
            pl.when(place != to)(lambda: flat_copy(to).start())
    else:
        reds[z] = mine
        lax.fori_loop(1, n, start(seq_copy), 0)
    later = iota(square, 0) <= iota(square, 1)
    d_decay = exact(jnp.where(later, 1.0, 0.0), d_cum)
    d_raw = cola[...] * ratio[...] - rate * slope * d_decay
    gdt_ref[...] = d_raw.T[0:heads, :]
    d_cb = jnp.where(causal, dcb[...], 0.0)
    gc_ref[...] = (gca[...] + mm(d_cb.astype(BF16), b16)).astype(BF16)
    gb_ref[...] = (gba[...] + mm(d_cb.T.astype(BF16), c16)).astype(BF16)
    if not flat:
        lax.fori_loop(1, n, finish(seq_copy), 0)
        redb[w] = lax.fori_loop(0, n, lambda i, t: t + reds[i], jnp.zeros((1, tokens), F32))
        lax.fori_loop(1, m, start(batch_copy), 0)

    @pl.when(z < n - 1)
    def _():
        pltpu.make_async_copy(fsend, fsend, fs_sem.at[0]).wait()

    @pl.when(z > 0)
    def _():
        pltpu.make_async_copy(bsend, bsend, bs_sem.at[0]).wait()

    if flat:
        flat_wait(rb_send.at[0])
        flat_wait(rb_recv.at[0])
    else:
        lax.fori_loop(1, m, finish(batch_copy), 0)
    total = jnp.sum(redb[...], axis=0)
    ga_out[...] = total[:, :heads]
    gbias_out[...] = turn(total, tokens - heads)[:, :heads]
    gskip_out[...] = turn(total, tokens - 2 * heads)[:, :heads]


def place_outputs(count, *refs):
    sems = refs[2 * count]
    copies = [
        pltpu.make_async_copy(refs[i], refs[count + i], sems.at[0]) for i in range(count)
    ]
    for copy in copies:
        copy.start()
    for copy in copies:
        copy.wait()


def shards(dt_raw, dt_bias, a_log, d_skip, x_in, b_in, c_in, cotangent):
    n, m = lax.axis_size("seq"), lax.axis_size("batch")
    _, tokens, heads = dt_raw.shape
    channels = x_in.shape[2]
    state = b_in.shape[2]
    chunks = channels // WIDTH
    steps = 1 if n * m <= FLAT else m - 1
    stops = 1 if n * m <= FLAT else 2 * (n - 1)
    groups = 1 + (chunks - 1) // (UNROLL if (chunks - 1) % UNROLL == 0 else 1)
    big = (chunks, tokens, WIDTH)
    square = (tokens, tokens)
    vmem = pl.BlockSpec(memory_space=pltpu.VMEM)
    hbm = pl.BlockSpec(memory_space=pltpu.HBM)
    dma = pltpu.SemaphoreType.DMA
    shape = jax.ShapeDtypeStruct
    made = pl.pallas_call(
        functools.partial(kernel, n, m, heads, tokens),
        out_shape=(
            shape((tokens, channels), BF16),
            shape((tokens, channels), BF16),
            shape((tokens, state), BF16),
            shape((tokens, state), BF16),
            shape((heads, tokens), F32),
        ) + (shape((1, heads), F32),) * 3,
        in_specs=[hbm] * 8,
        out_specs=(vmem,) * 8,
        scratch_shapes=[
            pltpu.VMEM((heads, tokens), F32),
            pltpu.VMEM((1, heads), F32),
            pltpu.VMEM((1, heads), F32),
            pltpu.VMEM((1, heads), F32),
            pltpu.VMEM((tokens, channels), BF16),
            pltpu.VMEM((tokens, state), BF16),
            pltpu.VMEM((tokens, state), BF16),
            pltpu.VMEM((tokens, channels), BF16),
            dma((6,)), dma((groups,)), dma((groups,)),
            pltpu.VMEM(square, F32),
            pltpu.VMEM((8, tokens), F32),
            pltpu.VMEM((2 * tokens + 16, tokens), BF16),
            pltpu.VMEM(square, BF16),
            pltpu.VMEM(square, F32),
            pltpu.VMEM((tokens, WIDTH), jnp.int32),
            pltpu.VMEM(square, F32),
            pltpu.VMEM((chunks, 8, WIDTH), F32),
            pltpu.VMEM(big, F32),
            pltpu.VMEM(big, F32),
            pltpu.VMEM(big, BF16),
            pltpu.VMEM(big, BF16),
            pltpu.VMEM(big, F32),
            pltpu.VMEM(big, F32),
            pltpu.VMEM(big, F32),
            pltpu.VMEM(big, F32),
            pltpu.VMEM(big, BF16),
            pltpu.VMEM(big, BF16),
            pltpu.VMEM(big, BF16),
            pltpu.VMEM(big, BF16),
            pltpu.VMEM(square, F32),
            pltpu.VMEM(square, F32),
            pltpu.VMEM(square, F32),
            pltpu.VMEM(square, F32),
            pltpu.VMEM(square, F32),
            pltpu.VMEM((8, tokens), F32),
            pltpu.VMEM(square, F32),
            pltpu.VMEM(square, F32),
            pltpu.VMEM(square, F32),
            pltpu.VMEM((n, 1, tokens), F32),
            pltpu.VMEM((n * m if n * m <= FLAT else m, 1, tokens), F32),
            dma((1,)), dma((chunks,)), dma((1,)), dma((chunks,)),
            dma((stops,)), dma((steps,)), dma((steps,)),
        ],
        compiler_params=pltpu.CompilerParams(
            collective_id=0, has_side_effects=True, vmem_limit_bytes=40 * 2**20),
    )(
        *(pltpu.with_memory_space_constraint(a, pltpu.HBM) for a in (
            dt_raw[0].T, dt_bias[None], a_log[None], d_skip[None],
            x_in[0], b_in[0], c_in[0], cotangent[0]))
    )
    out, gx, gb, gc, gdt, alog, bias, skip = pl.pallas_call(
        functools.partial(place_outputs, 8),
        out_shape=tuple(shape(a.shape, a.dtype) for a in made),
        in_specs=[vmem] * 8,
        out_specs=(hbm,) * 8,
        scratch_shapes=[dma((1,))],
        compiler_params=pltpu.CompilerParams(vmem_limit_bytes=4 * 2**20),
    )(*made)
    return (out[None], gx[None], gb[None], gc[None], gdt.T[None], alog[0], bias[0], skip[0])


def solution(mesh):
    rows = P("batch", "seq", None)
    return jax.shard_map(
        shards,
        mesh=mesh,
        in_specs=(rows, P(), P(), P(), rows, rows, rows, rows),
        out_specs=(rows, rows, rows, rows, rows, P(), P(), P()),
        check_vma=False,
    )
```
